128 devices in a mesh: rows: 16 (over x, z_hi, core), cols: 8 (over z_lo, y).
Axes of the slice: x: 4, y: 4, z: 4 (z_hi: 2, z_lo: 2; z = z_hi * 2 + z_lo), core: 2. Of those that a mesh axis runs over, the one named last changes fastest.
Arguments:
- stem_strips: bfloat16 [768, 512, 256], P(('rows', 'cols')), may hold values from -6 to 6
- norm_scale: float32 [256], replicated, may hold values from 0.1 to 1.9
- norm_shift: float32 [256], replicated, may hold values from -3 to 3
- expand_weight: bfloat16 [256, 1024], replicated, may hold values from -0.375 to 0.375
- depth_weight: float32 [9, 1024], replicated, may hold values from -2 to 2
- project_weight: bfloat16 [1024, 256], replicated, may hold values from -0.1875 to 0.1875
- block_gain: float32 [256], replicated, may hold values from 0.1 to 1.9
- block_inputs: bfloat16 [256, 768], replicated, may hold values from -0.375 to 0.375
- block_output: bfloat16 [256, 256], replicated, may hold values from -0.375 to 0.375
- block_bias: float32 [8, 64, 64], replicated, may hold values from -4 to 300, as said below
- first_gain: float32 [256], replicated, may hold values from 0.1 to 1.9
- first_up: bfloat16 [256, 1024], replicated, may hold values from -0.375 to 0.375
- first_down: bfloat16 [1024, 256], replicated, may hold values from -0.1875 to 0.1875
- grid_gain: float32 [256], replicated, may hold values from 0.1 to 1.9
- grid_inputs: bfloat16 [256, 768], replicated, may hold values from -0.375 to 0.375
- grid_output: bfloat16 [256, 256], replicated, may hold values from -0.375 to 0.375
- grid_bias: float32 [8, 64, 64], replicated, may hold values from -4 to 300, as said below
- second_gain: float32 [256], replicated, may hold values from 0.1 to 1.9
- second_up: bfloat16 [256, 1024], replicated, may hold values from -0.375 to 0.375
- second_down: bfloat16 [1024, 256], replicated, may hold values from -0.1875 to 0.1875
Outputs:
- block_out: bfloat16 [768, 512, 256], P('rows', 'cols')
The draws below stay inside these ranges and needn't reach their ends.
Inputs may be any that keep to these rules, and one draw needn't show every extreme that they name: `block_bias`: entries of the position bias table. `grid_bias`: entries of the position bias table.
All inputs are finite; a program needn't handle non-finite values.
Results may differ from the reference program's by a relative error of at most 0.018.
Values may be sent and summed in bfloat16 or wider, within the bound.
No kernel may reach another device: no remote copies, remote signals or barrier semaphores. Data moves between devices by JAX's collectives and lax.ppermute only.
A program may use at most 128 MiB of HBM per device.

```python
import jax
import jax.numpy as jnp
from jax import lax

CHANNELS = 256
EXPAND = 1024
MLP_HIDDEN = 1024
HEADS = 8
HEIGHT = 768
WIDTH = 512


def base_table(key):
    table = jax.random.normal(key, (HEADS, 64, 64), jnp.float32)
    return jnp.clip(table, -4.0, 4.0)


def draw_block_bias(key, part):
    key = jax.random.fold_in(key, 11)
    table = base_table(key)
    return table


def draw_grid_bias(key, part):
    key = jax.random.fold_in(key, 23)
    table = base_table(key)
    return table


def level_of(rng, shape, cuts, smallest, top_value):
    factor_of, own = 1.0, jax.random.fold_in(rng, 6)
    for dim, parts in cuts:
        heights = jnp.exp(jax.random.uniform(jax.random.fold_in(own, dim), (parts,), jnp.float32, smallest / len(cuts), top_value / len(cuts)))
        factor_of = factor_of * jnp.repeat(heights, shape[dim] // parts).reshape([-1 if axis == dim else 1 for axis in range(len(shape))])
    return factor_of


def scatter_about(stream_key, dims, scale, most, cuts=(), dtype=jnp.bfloat16):
    values = jax.random.normal(stream_key, dims, jnp.float32) * scale
    if len(cuts) > 0:
        values = level_of(stream_key, dims, cuts, -0.22, 0.18) * values
    return jnp.clip(values, min=-most, max=most).astype(dtype)


def setup_inputs(seed: int = 0) -> dict:
    splits = jax.random.split(jax.random.key(seed), 21)
    stem_strips = scatter_about(splits[0], (HEIGHT, WIDTH, CHANNELS), 1.0, 6.0, ((0, 128),))
    norm_scale = jnp.clip(1.0 + 0.18 * jax.random.normal(splits[1], (CHANNELS,), jnp.float32), 0.1, 1.9)
    norm_shift = scatter_about(splits[2], (CHANNELS,), 0.5, 3.0, (), jnp.float32)
    expand_weight = scatter_about(splits[3], (CHANNELS, EXPAND), CHANNELS ** -0.5, 0.375)
    depth_weight = scatter_about(splits[4], (9, EXPAND), 9 ** -0.5, 2.0, (), jnp.float32)
    project_weight = scatter_about(splits[5], (EXPAND, CHANNELS), EXPAND ** -0.5, 0.1875)
    block_gain = jnp.clip(1.0 + 0.18 * jax.random.normal(splits[6], (CHANNELS,), jnp.float32), 0.1, 1.9)
    block_inputs = scatter_about(splits[7], (CHANNELS, 3 * CHANNELS), CHANNELS ** -0.5, 0.375)
    block_output = scatter_about(splits[8], (CHANNELS, CHANNELS), CHANNELS ** -0.5, 0.375)
    block_bias = draw_block_bias(jax.random.fold_in(splits[20], 71), 0)
    first_gain = jnp.clip(1.0 + 0.18 * jax.random.normal(splits[10], (CHANNELS,), jnp.float32), 0.1, 1.9)
    first_up = scatter_about(splits[11], (CHANNELS, MLP_HIDDEN), CHANNELS ** -0.5, 0.375)
    first_down = scatter_about(splits[12], (MLP_HIDDEN, CHANNELS), MLP_HIDDEN ** -0.5, 0.1875)
    grid_gain = jnp.clip(1.0 + 0.18 * jax.random.normal(splits[13], (CHANNELS,), jnp.float32), 0.1, 1.9)
    grid_inputs = scatter_about(splits[14], (CHANNELS, 3 * CHANNELS), CHANNELS ** -0.5, 0.375)
    grid_output = scatter_about(splits[15], (CHANNELS, CHANNELS), CHANNELS ** -0.5, 0.375)
    grid_bias = draw_grid_bias(jax.random.fold_in(splits[20], 71), 0)
    second_gain = jnp.clip(1.0 + 0.18 * jax.random.normal(splits[17], (CHANNELS,), jnp.float32), 0.1, 1.9)
    second_up = scatter_about(splits[18], (CHANNELS, MLP_HIDDEN), CHANNELS ** -0.5, 0.375)
    second_down = scatter_about(splits[19], (MLP_HIDDEN, CHANNELS), MLP_HIDDEN ** -0.5, 0.1875)
    return {"stem_strips": stem_strips, "norm_scale": norm_scale, "norm_shift": norm_shift, "expand_weight": expand_weight, "depth_weight": depth_weight, "project_weight": project_weight, "block_gain": block_gain, "block_inputs": block_inputs, "block_output": block_output, "block_bias": block_bias, "first_gain": first_gain, "first_up": first_up, "first_down": first_down, "grid_gain": grid_gain, "grid_inputs": grid_inputs, "grid_output": grid_output, "grid_bias": grid_bias, "second_gain": second_gain, "second_up": second_up, "second_down": second_down}


EPSILON = 1e-05

def layer_norm(values, norm_gain):
    values = values.astype(jnp.float32)
    center = values - lax.optimization_barrier(jnp.mean(values, axis=-1, keepdims=True))
    spread = lax.optimization_barrier(jnp.mean(center * center, axis=-1, keepdims=True))
    return (center * lax.rsqrt(spread + EPSILON) * norm_gain).astype(jnp.bfloat16)

def attend(windows, norm_gain, in_weight, out_weight, pos_bias):
    count_win, places, channels = windows.shape
    head_count = pos_bias.shape[0]
    head_width = channels // head_count
    normed = layer_norm(windows.reshape(-1, channels), norm_gain)
    packed = jnp.dot(normed, in_weight, preferred_element_type=jnp.float32).astype(jnp.bfloat16)
    packed = packed.reshape(count_win, places, 3, head_count, head_width).astype(jnp.float32)
    queries = packed[:, :, 0]
    key_part = packed[:, :, 1]
    val_part = packed[:, :, 2]
    scores = jnp.einsum('wqhd,wkhd->whqk', queries, key_part) * head_width ** (-0.5) + pos_bias
    scores = scores - lax.optimization_barrier(jnp.max(scores, axis=-1, keepdims=True))
    attention = jnp.exp(scores)
    attention = (attention / lax.optimization_barrier(jnp.sum(attention, axis=-1, keepdims=True))).astype(jnp.bfloat16)
    combined = jnp.einsum('whqk,wkhd->wqhd', attention.astype(jnp.float32), val_part).astype(jnp.bfloat16)
    update = jnp.dot(combined.reshape(-1, channels), out_weight, preferred_element_type=jnp.float32)
    result = windows.reshape(-1, channels).astype(jnp.float32) + update
    return result.astype(jnp.bfloat16).reshape(count_win, places, channels)

def feed_forward(tokens, norm_gain, up_weight, down_weight):
    normed = layer_norm(tokens, norm_gain)
    hidden = jax.nn.gelu(jnp.dot(normed, up_weight, preferred_element_type=jnp.float32)).astype(jnp.bfloat16)
    result = tokens.astype(jnp.float32) + jnp.dot(hidden, down_weight, preferred_element_type=jnp.float32)
    return result.astype(jnp.bfloat16)

def bottleneck(frame_in, norm_scale, norm_shift, expand_weight, depth_weight, project_weight):
    height_px, width_px, channels = frame_in.shape
    wide = expand_weight.shape[1]
    band_rows = 8
    normed = (frame_in.astype(jnp.float32) * norm_scale + norm_shift).astype(jnp.bfloat16)

    def expand_band(rows_in):
        flat = jnp.dot(rows_in.reshape(-1, channels), expand_weight, preferred_element_type=jnp.float32)
        return jax.nn.gelu(flat).astype(jnp.bfloat16).reshape(band_rows, width_px, wide)
    expanded = lax.map(expand_band, normed.reshape(height_px // band_rows, band_rows, width_px, channels))
    expanded = expanded.reshape(height_px, width_px, wide)
    padded = jnp.pad(expanded, ((1, 1), (1, 1), (0, 0)))

    def depth_band(start_row):
        window = lax.dynamic_slice_in_dim(padded, start_row, band_rows + 2, 0)
        running = jnp.zeros((band_rows, width_px, wide), jnp.float32)
        for offset in range(9):
            shifted = window[offset // 3:offset // 3 + band_rows, offset % 3:offset % 3 + width_px]
            running = running + shifted.astype(jnp.float32) * depth_weight[offset]
        activated = jax.nn.gelu(running).astype(jnp.bfloat16)
        flat = jnp.dot(activated.reshape(-1, wide), project_weight, preferred_element_type=jnp.float32)
        return flat.reshape(band_rows, width_px, channels)
    starts = (jnp.arange(height_px // band_rows) * band_rows).astype(jnp.int32)
    update = lax.map(depth_band, starts).reshape(height_px, width_px, channels)
    return (frame_in.astype(jnp.float32) + update).astype(jnp.bfloat16)

def section_windows(windows, norm_gain, in_weight, out_weight, pos_bias, mlp_gain, up_weight, down_weight):
    count_win, places, channels = windows.shape
    group = 32

    def one_group(block):
        attended = attend(block, norm_gain, in_weight, out_weight, pos_bias)
        mixed_out = feed_forward(attended.reshape(-1, channels), mlp_gain, up_weight, down_weight)
        return mixed_out.reshape(group, places, channels)
    result = lax.map(one_group, windows.reshape(count_win // group, group, places, channels))
    return result.reshape(count_win, places, channels)

def reference(stem_strips, norm_scale, norm_shift, expand_weight, depth_weight, project_weight, block_gain, block_inputs, block_output, block_bias, first_gain, first_up, first_down, grid_gain, grid_inputs, grid_output, grid_bias, second_gain, second_up, second_down):
    height_px, width_px, channels = stem_strips.shape
    section1 = bottleneck(stem_strips, norm_scale, norm_shift, expand_weight, depth_weight, project_weight)
    blocks = section1.reshape(height_px // 8, 8, width_px // 8, 8, channels).transpose(0, 2, 1, 3, 4)
    blocks = blocks.reshape(-1, 64, channels)
    blocks = section_windows(blocks, block_gain, block_inputs, block_output, block_bias, first_gain, first_up, first_down)
    section3 = blocks.reshape(height_px // 8, width_px // 8, 8, 8, channels).transpose(0, 2, 1, 3, 4)
    section3 = section3.reshape(height_px, width_px, channels)
    grids = section3.reshape(8, height_px // 8, 8, width_px // 8, channels).transpose(1, 3, 0, 2, 4)
    grids = grids.reshape(-1, 64, channels)
    grids = section_windows(grids, grid_gain, grid_inputs, grid_output, grid_bias, second_gain, second_up, second_down)
    result = grids.reshape(height_px // 8, width_px // 8, 8, 8, channels).transpose(2, 0, 3, 1, 4)
    return result.reshape(height_px, width_px, channels)
```

```python
import functools

import jax
import jax.numpy as jnp
from jax import lax
from jax.experimental import pallas as pl
from jax.experimental.pallas import tpu as pltpu
from jax.sharding import PartitionSpec as P

EPSILON = 1e-05
LOG2E = 1.4426950408889634
GELU_A = 0.7978845608028654
GELU_B = GELU_A * 0.044715
VMEM_LIMIT = 56 * 1024 * 1024
F32 = jnp.float32
BF16 = jnp.bfloat16

CORE_ROWS = [[core + 2 * i for i in range(8)] for core in range(2)]
CORE_ALL = [[(core + 2 * i) * 8 + c for i in range(8) for c in range(8)] for core in range(2)]
Y_UP = [(c, c + 1) for c in range(7) if c % 4 != 3]
Y_DOWN = [(c + 1, c) for c in range(7) if c % 4 != 3]


def twice_gelu(x):
    inner = x * (GELU_B * (x * x) + GELU_A)
    return x * (1.0 + jnp.tanh(inner))


def own_y():
    return lax.rem(lax.axis_index("cols"), 4)


def bottleneck_kernel(
    x_ref, top_ref, bot_ref, scale_ref, shift_ref, we_ref, dw_ref, wp_ref,
    own_ref, up_ref, down_ref, e_ref,
):
    device = lax.axis_index("rows") * 8 + lax.axis_index("cols")
    has_top = (device > 0).astype(F32)
    has_bot = (device < 127).astype(F32)
    scale = scale_ref[...]
    shift = shift_ref[...]
    pad = 8

    edge = jnp.zeros((pad, 128), F32)

    def clear(index, carry):
        for lb in range(8):
            e_ref[index, lb, 0:pad, :] = edge
            e_ref[index, lb, 512 + pad : 512 + 2 * pad, :] = edge
        return carry

    lax.fori_loop(0, 8, clear, 0)

    def expand(values, row, ct, factor):
        normed = (values.astype(F32) * scale + shift).astype(BF16)
        start = pl.multiple_of(ct * 128, 128) + pad
        for nb in range(4):
            flat = jnp.dot(
                normed, we_ref[:, nb * 256 : (nb + 1) * 256], preferred_element_type=F32
            )
            wide = twice_gelu(flat)
            if factor is not None:
                wide = wide * factor
            for half in range(2):
                e_ref[row, nb * 2 + half, pl.ds(start, 128), :] = wide[
                    :, half * 128 : (half + 1) * 128
                ]

    def expand_own(step, carry):
        row = step // 4
        ct = lax.rem(step, 4)
        expand(x_ref[row, pl.ds(pl.multiple_of(ct * 128, 128), 128), :], row + 1, ct, None)
        return carry

    def expand_edge(ct, carry):
        cols = pl.ds(pl.multiple_of(ct * 128, 128), 128)
        expand(top_ref[0, cols, :], 0, ct, has_top)
        expand(bot_ref[0, cols, :], 7, ct, has_bot)
        return carry

    lax.fori_loop(0, 24, expand_own, 0)
    lax.fori_loop(0, 4, expand_edge, 0)

    def depth(step, carry):
        row = step // 4
        ct = lax.rem(step, 4)
        base = pl.multiple_of(ct * 128, 128)
        total = jnp.zeros((128, 256), F32)
        for pair in range(4):
            parts = []
            for lb in (2 * pair, 2 * pair + 1):
                acc = None
                for tap in range(9):
                    term = (
                        e_ref[row + tap // 3, lb, pl.ds(base + (pad - 1 + tap % 3), 128), :]
                        * dw_ref[tap : tap + 1, lb * 128 : (lb + 1) * 128]
                    )
                    acc = term if acc is None else acc + term
                parts.append(twice_gelu(acc).astype(BF16))
            wide = jnp.concatenate(parts, axis=1)
            total = total + jnp.dot(
                wide, wp_ref[pair * 256 : (pair + 1) * 256, :], preferred_element_type=F32
            )
        result = x_ref[row, pl.ds(base, 128), :].astype(F32) + 0.5 * total
        result = result.astype(BF16)
        for jj in range(2):
            for tp in range(4):
                at = jj * 64 + tp * 16
                own_ref[row * 4 + tp, ct * 2 + jj] = result[at : at + 16]
        return carry

    lax.fori_loop(0, 24, depth, 0)

    y = own_y()

    def pick(m, carry):
        n_up = y + 1
        row = jnp.minimum(2 * y + m // n_up, 5)
        up_ref[m] = own_ref[row * 4 + 3 - y + lax.rem(m, n_up)]
        n_down = 4 - y
        row = jnp.minimum(m // n_down, 5)
        down_ref[m] = own_ref[row * 4 + lax.rem(m, n_down)]
        return carry

    lax.fori_loop(0, 8, pick, 0)


def bottleneck(strips, top, bot, scale, shift, we, dw, wp):
    return pl.pallas_call(
        bottleneck_kernel,
        out_shape=[
            jax.ShapeDtypeStruct((24, 8, 16, 256), BF16),
            jax.ShapeDtypeStruct((8, 8, 16, 256), BF16),
            jax.ShapeDtypeStruct((8, 8, 16, 256), BF16),
        ],
        scratch_shapes=[pltpu.VMEM((8, 8, 528, 128), F32)],
        compiler_params=pltpu.CompilerParams(vmem_limit_bytes=VMEM_LIMIT),
        name="bottleneck",
    )(strips, top, bot, scale, shift, we, dw, wp)


def normed_of(x, gain):
    center = x - jnp.mean(x, axis=-1, keepdims=True)
    spread = jnp.mean(center * center, axis=-1, keepdims=True)
    return (center * lax.rsqrt(spread + EPSILON) * gain).astype(BF16)


def head_masks(dtype):
    lane = lax.broadcasted_iota(jnp.int32, (1, 128), 1)
    return [(lane // 32 == h).astype(F32).astype(dtype) for h in range(4)]


def attend_and_mix(x, w):
    tokens = x.shape[0]
    masks = head_masks(BF16)
    masks_f = head_masks(F32)
    normed = normed_of(x, w["gain_a"][...])
    q, k, v = [
        jnp.dot(normed, w["inputs"][:, c * 256 : (c + 1) * 256], preferred_element_type=F32).astype(
            BF16
        )
        for c in range(3)
    ]
    rows = []
    for win in range(tokens // 64):
        at = slice(win * 64, (win + 1) * 64)
        groups = []
        for g in range(2):
            lanes = slice(g * 128, (g + 1) * 128)
            qg, kg, vg = q[at, lanes], k[at, lanes], v[at, lanes]
            spread_q = jnp.concatenate([qg * masks[h] for h in range(4)], axis=0)
            scores = lax.dot_general(
                kg, spread_q, (((1,), (1,)), ((), ())), preferred_element_type=F32
            )
            scores = scores * (LOG2E * 32**-0.5) + w["bias"][g]
            scores = scores - jnp.max(scores, axis=0, keepdims=True)
            weights = jnp.exp2(scores)
            weights = weights * (1.0 / jnp.sum(weights, axis=0, keepdims=True))
            mixed = lax.dot_general(
                weights.astype(BF16), vg, (((0,), (0,)), ((), ())), preferred_element_type=F32
            )
            out = mixed[0:64] * masks_f[0]
            for h in range(1, 4):
                out = out + mixed[h * 64 : (h + 1) * 64] * masks_f[h]
            groups.append(out.astype(BF16))
        rows.append(jnp.concatenate(groups, axis=1))
    combined = jnp.concatenate(rows, axis=0)
    x = x + jnp.dot(combined, w["output"][...], preferred_element_type=F32)
    x = x.astype(BF16).astype(F32)
    normed = normed_of(x, w["gain_m"][...])
    total = jnp.zeros((tokens, 256), F32)
    for c in range(4):
        cols = slice(c * 256, (c + 1) * 256)
        hidden = jnp.dot(normed, w["up"][:, cols], preferred_element_type=F32)
        hidden = twice_gelu(hidden).astype(BF16)
        total = total + jnp.dot(hidden, w["down"][cols, :], preferred_element_type=F32)
    return x + 0.5 * total


NAMES = ("gain_a", "inputs", "output", "bias", "gain_m", "up", "down")


def block_kernel(k, own_ref, up_ref, down_ref, *refs):
    w = dict(zip(NAMES, refs))
    out_ref = refs[len(NAMES)]
    y = own_y()
    n = 3 * y + k
    p = n // 4
    tp = lax.rem(n, 4)
    places = []
    for s in range(8):
        row = 8 * p + s
        owner = row // 6
        local = row - 6 * owner
        v = jnp.maximum(y - 1, 0)
        m_up = jnp.clip((local - 2 * v) * (v + 1) + tp - (3 - v), 0, 7)
        v = jnp.minimum(y + 1, 3)
        m_down = jnp.clip(local * (4 - v) + tp, 0, 7)
        places.append((owner, local * 4 + tp, m_up, m_down))

    def step(g, carry):
        units = []
        for owner, at, m_up, m_down in places:
            js = pl.ds(g * 2, 2)
            mine = own_ref[at, js].astype(F32)
            above = up_ref[m_up, js].astype(F32)
            below = down_ref[m_down, js].astype(F32)
            units.append(jnp.where(owner == y, mine, jnp.where(owner < y, above, below)))
        x = jnp.concatenate(
            [
                units[s][jj, t * 8 : (t + 1) * 8, :]
                for jj in range(2)
                for t in range(2)
                for s in range(8)
            ],
            axis=0,
        )
        out = attend_and_mix(x, w)
        for s in range(8):
            for jj in range(2):
                both = [out[(jj * 2 + t) * 64 + s * 8 :][:8] for t in range(2)]
                out_ref[s, g * 2 + jj] = jnp.concatenate(both, axis=0).astype(BF16)
        return carry

    lax.fori_loop(0, 4, step, 0)


def grid_kernel(x_ref, *refs):
    w = dict(zip(NAMES, refs))
    out_ref, flat_ref = refs[len(NAMES) :]

    def load(i, carry):
        values = x_ref[i].astype(F32).reshape(128, 256)
        for half in range(2):
            flat_ref[half, pl.ds(pl.multiple_of(i * 128, 128), 128), :] = values[
                :, half * 128 : (half + 1) * 128
            ]
        return carry

    lax.fori_loop(0, 8, load, 0)

    def step(g, carry):
        windows = []
        for b in range(4):
            at = pl.ds(g * 4 + b, 64, stride=16)
            windows.append(
                jnp.concatenate([flat_ref[half, at, :] for half in range(2)], axis=1)
            )
        out = attend_and_mix(jnp.concatenate(windows, axis=0), w)
        for b in range(4):
            at = pl.ds(g * 4 + b, 64, stride=16)
            for half in range(2):
                flat_ref[half, at, :] = out[
                    b * 64 : (b + 1) * 64, half * 128 : (half + 1) * 128
                ]
        return carry

    lax.fori_loop(0, 4, step, 0)

    def store(i, carry):
        at = pl.ds(pl.multiple_of(i * 128, 128), 128)
        values = jnp.concatenate([flat_ref[half, at, :] for half in range(2)], axis=1)
        out_ref[pl.ds(i * 8, 8)] = values.astype(BF16).reshape(8, 16, 256)
        return carry

    lax.fori_loop(0, 8, store, 0)


def block_section(k, own, up, down, weights):
    return pl.pallas_call(
        functools.partial(block_kernel, k),
        out_shape=jax.ShapeDtypeStruct((8, 8, 16, 256), BF16),
        compiler_params=pltpu.CompilerParams(vmem_limit_bytes=VMEM_LIMIT),
        name="block_section",
    )(own, up, down, *weights)


def grid_section(x, weights):
    return pl.pallas_call(
        grid_kernel,
        out_shape=jax.ShapeDtypeStruct((64, 16, 256), BF16),
        scratch_shapes=[pltpu.VMEM((2, 1024, 128), F32)],
        compiler_params=pltpu.CompilerParams(vmem_limit_bytes=VMEM_LIMIT),
        name="grid_section",
    )(x, *weights)


def turned_bias(bias):
    return (bias * LOG2E).reshape(2, 4, 64, 64).transpose(0, 3, 1, 2).reshape(2, 64, 256)


def body(
    stem_strips, norm_scale, norm_shift, expand_weight, depth_weight, project_weight,
    block_gain, block_inputs, block_output, block_bias, first_gain, first_up, first_down,
    grid_gain, grid_inputs, grid_output, grid_bias, second_gain, second_up, second_down,
):
    row = lambda a: a.reshape(1, -1)
    both = ("rows", "cols")
    top = lax.ppermute(stem_strips[5:6], both, [(d, d + 1) for d in range(127)])
    bot = lax.ppermute(stem_strips[0:1], both, [(d + 1, d) for d in range(127)])
    own, up, down = bottleneck(
        stem_strips, top, bot, row(norm_scale), row(norm_shift), expand_weight,
        depth_weight * 0.5, project_weight,
    )
    up = lax.ppermute(up, "cols", Y_UP)
    down = lax.ppermute(down, "cols", Y_DOWN)
    block_weights = (
        row(block_gain), block_inputs, block_output, turned_bias(block_bias),
        row(first_gain), first_up, first_down,
    )
    grid_weights = (
        row(grid_gain), grid_inputs, grid_output, turned_bias(grid_bias),
        row(second_gain), second_up, second_down,
    )
    done = [block_section(k, own, up, down, block_weights) for k in range(3)]
    sent = jnp.stack(done, axis=1)
    arrived = lax.all_to_all(sent, "rows", 0, 0, axis_index_groups=CORE_ROWS, tiled=True)
    grids = [grid_section(arrived[:, k], grid_weights) for k in range(3)]
    back = jnp.stack(grids, axis=1)
    landed = lax.all_to_all(back, both, 0, 0, axis_index_groups=CORE_ALL, tiled=True)
    landed = landed.reshape(8, 2, 3, 4, 16, 256).transpose(1, 2, 0, 3, 4, 5)
    return landed.reshape(48, 64, 256)


def solution(mesh):
    return jax.shard_map(
        body,
        mesh=mesh,
        in_specs=(P(("rows", "cols"), None, None),) + (P(),) * 19,
        out_specs=P("rows", "cols", None),
        check_vma=False,
    )
```

```python
import functools

import jax
import jax.numpy as jnp
from jax import lax
from jax.experimental import pallas as pl
from jax.experimental.pallas import tpu as pltpu
from jax.sharding import PartitionSpec as P

EPSILON = 1e-05
LOG2E = 1.4426950408889634
GELU_A = 0.7978845608028654
GELU_B = GELU_A * 0.044715
VMEM_LIMIT = 40 * 1024 * 1024
F32 = jnp.float32
BF16 = jnp.bfloat16

CORE_ROWS = [[core + 2 * i for i in range(8)] for core in range(2)]
CORE_ALL = [[(core + 2 * i) * 8 + c for i in range(8) for c in range(8)] for core in range(2)]
Y_UP = [(c, c + 1) for c in range(7) if c % 4 != 3]
Y_DOWN = [(c + 1, c) for c in range(7) if c % 4 != 3]


def twice_gelu(x):
    inner = x * (GELU_B * (x * x) + GELU_A)
    return x * (1.0 + jnp.tanh(inner))


def own_y():
    return lax.rem(lax.axis_index("cols"), 4)


def bottleneck_kernel(
    x_ref, top_ref, bot_ref, scale_ref, shift_ref, we_ref, dw_ref, wp_ref,
    own_ref, up_ref, down_ref, e_ref,
):
    device = lax.axis_index("rows") * 8 + lax.axis_index("cols")
    has_top = (device > 0).astype(F32)
    has_bot = (device < 127).astype(F32)
    scale = scale_ref[...]
    shift = shift_ref[...]
    pad = 8

    edge = jnp.zeros((pad, 128), F32)

    def clear(index, carry):
        for lb in range(8):
            e_ref[index, lb, 0:pad, :] = edge
            e_ref[index, lb, 512 + pad : 512 + 2 * pad, :] = edge
        return carry

    lax.fori_loop(0, 8, clear, 0)

    def expand(values, row, factor):
        normed = (values.astype(F32) * scale + shift).astype(BF16)
        for nb in range(4):
            flat = jnp.dot(
                normed, we_ref[:, nb * 256 : (nb + 1) * 256], preferred_element_type=F32
            )
            wide = twice_gelu(flat)
            if factor is not None:
                wide = wide * factor
            for half in range(2):
                e_ref[row, nb * 2 + half, pad : 512 + pad, :] = wide[
                    :, half * 128 : (half + 1) * 128
                ]

    def expand_own(row, carry):
        expand(x_ref[row], row + 1, None)
        return carry

    lax.fori_loop(0, 6, expand_own, 0)
    expand(top_ref[0], 0, has_top)
    expand(bot_ref[0], 7, has_bot)
    taps = dw_ref[...] * 0.5

    def depth(row, carry):
        total = jnp.zeros((512, 256), F32)
        for pair in range(4):
            parts = []
            for lb in (2 * pair, 2 * pair + 1):
                acc = None
                for tap in range(9):
                    term = (
                        e_ref[row + tap // 3, lb, pl.ds(pad - 1 + tap % 3, 512), :]
                        * taps[tap : tap + 1, lb * 128 : (lb + 1) * 128]
                    )
                    acc = term if acc is None else acc + term
                parts.append(twice_gelu(acc).astype(BF16))
            wide = jnp.concatenate(parts, axis=1)
            total = total + jnp.dot(
                wide, wp_ref[pair * 256 : (pair + 1) * 256, :], preferred_element_type=F32
            )
        result = x_ref[row].astype(F32) + 0.5 * total
        result = result.astype(BF16)
        for jj in range(8):
            for tp in range(4):
                at = jj * 64 + tp * 16
                own_ref[row * 4 + tp, jj] = result[at : at + 16]
        return carry

    lax.fori_loop(0, 6, depth, 0)

    y = own_y()

    def pick(m, carry):
        n_up = y + 1
        row = jnp.minimum(2 * y + m // n_up, 5)
        up_ref[m] = own_ref[row * 4 + 3 - y + lax.rem(m, n_up)]
        n_down = 4 - y
        row = jnp.minimum(m // n_down, 5)
        down_ref[m] = own_ref[row * 4 + lax.rem(m, n_down)]
        return carry

    lax.fori_loop(0, 8, pick, 0)


def bottleneck(strips, top, bot, scale, shift, we, dw, wp):
    return pl.pallas_call(
        bottleneck_kernel,
        out_shape=[
            jax.ShapeDtypeStruct((24, 8, 16, 256), BF16),
            jax.ShapeDtypeStruct((8, 8, 16, 256), BF16),
            jax.ShapeDtypeStruct((8, 8, 16, 256), BF16),
        ],
        scratch_shapes=[pltpu.VMEM((8, 8, 528, 128), F32)],
        compiler_params=pltpu.CompilerParams(vmem_limit_bytes=VMEM_LIMIT),
        name="bottleneck",
    )(strips, top, bot, scale, shift, we, dw, wp)


def normed_of(x, gain):
    center = x - jnp.mean(x, axis=-1, keepdims=True)
    spread = jnp.mean(center * center, axis=-1, keepdims=True)
    return (center * lax.rsqrt(spread + EPSILON) * gain).astype(BF16)


def head_masks(dtype):
    lane = lax.broadcasted_iota(jnp.int32, (1, 128), 1)
    return [(lane // 32 == h).astype(F32).astype(dtype) for h in range(4)]


def attend_and_mix(x, w):
    tokens = x.shape[0]
    masks = head_masks(BF16)
    key_head = lax.broadcasted_iota(jnp.int32, (256, 128), 0) // 64
    lane_head = lax.broadcasted_iota(jnp.int32, (256, 128), 1) // 32
    head_ones = (key_head == lane_head).astype(F32).astype(BF16)
    score_lane = lax.broadcasted_iota(jnp.int32, (64, 256), 1)
    bias = [
        jnp.concatenate([w["bias"][4 * g + h] for h in range(4)], axis=1) * LOG2E
        for g in range(2)
    ]
    normed = normed_of(x, w["gain_a"][...])
    q, k, v = [
        jnp.dot(normed, w["inputs"][:, c * 256 : (c + 1) * 256], preferred_element_type=F32).astype(
            BF16
        )
        for c in range(3)
    ]
    rows = []
    for win in range(tokens // 64):
        at = slice(win * 64, (win + 1) * 64)
        groups = []
        for g in range(2):
            lanes = slice(g * 128, (g + 1) * 128)
            qg, kg, vg = q[at, lanes], k[at, lanes], v[at, lanes]
            keys = jnp.concatenate([kg * masks[h] for h in range(4)], axis=0)
            values = jnp.concatenate([vg * masks[h] for h in range(4)], axis=0)
            values = jnp.concatenate([values, head_ones], axis=1)
            scores = lax.dot_general(
                qg, keys, (((1,), (1,)), ((), ())), preferred_element_type=F32
            )
            scores = scores * (LOG2E * 32**-0.5) + bias[g]
            top = None
            for h in range(4):
                peak = jnp.max(scores[:, h * 64 : (h + 1) * 64], axis=1, keepdims=True)
                top = (
                    jnp.broadcast_to(peak, (64, 256))
                    if top is None
                    else jnp.where(score_lane >= h * 64, peak, top)
                )
            weights = jnp.exp2(scores - top).astype(BF16)
            mixed = jnp.dot(weights, values, preferred_element_type=F32)
            groups.append((mixed[:, :128] * (1.0 / mixed[:, 128:])).astype(BF16))
        rows.append(jnp.concatenate(groups, axis=1))
    combined = jnp.concatenate(rows, axis=0)
    x = x + jnp.dot(combined, w["output"][...], preferred_element_type=F32)
    x = x.astype(BF16).astype(F32)
    normed = normed_of(x, w["gain_m"][...])
    total = jnp.zeros((tokens, 256), F32)
    for c in range(4):
        cols = slice(c * 256, (c + 1) * 256)
        hidden = jnp.dot(normed, w["up"][:, cols], preferred_element_type=F32)
        hidden = twice_gelu(hidden).astype(BF16)
        total = total + jnp.dot(hidden, w["down"][cols, :], preferred_element_type=F32)
    return x + 0.5 * total


NAMES = ("gain_a", "inputs", "output", "bias", "gain_m", "up", "down")


def block_kernel(k, own_ref, up_ref, down_ref, *refs):
    w = dict(zip(NAMES, refs))
    out_ref = refs[len(NAMES)]
    y = own_y()
    n = 3 * y + k
    p = n // 4
    tp = lax.rem(n, 4)
    places = []
    for s in range(8):
        row = 8 * p + s
        owner = row // 6
        local = row - 6 * owner
        v = jnp.maximum(y - 1, 0)
        m_up = jnp.clip((local - 2 * v) * (v + 1) + tp - (3 - v), 0, 7)
        v = jnp.minimum(y + 1, 3)
        m_down = jnp.clip(local * (4 - v) + tp, 0, 7)
        places.append((owner, local * 4 + tp, m_up, m_down))

    def step(g, carry):
        units = []
        for owner, at, m_up, m_down in places:
            js = pl.ds(g * 8, 8)
            mine = own_ref[at, js].astype(F32)
            above = up_ref[m_up, js].astype(F32)
            below = down_ref[m_down, js].astype(F32)
            units.append(jnp.where(owner == y, mine, jnp.where(owner < y, above, below)))
        x = jnp.concatenate(
            [
                units[s][jj, t * 8 : (t + 1) * 8, :]
                for jj in range(8)
                for t in range(2)
                for s in range(8)
            ],
            axis=0,
        )
        out = attend_and_mix(x, w)
        for s in range(8):
            for jj in range(8):
                both = [out[(jj * 2 + t) * 64 + s * 8 :][:8] for t in range(2)]
                out_ref[s, g * 8 + jj] = jnp.concatenate(both, axis=0).astype(BF16)
        return carry

    step(0, 0)


def grid_kernel(x_ref, *refs):
    w = dict(zip(NAMES, refs))
    out_ref, flat_ref = refs[len(NAMES) :]

    def load(i, carry):
        values = x_ref[i].astype(F32).reshape(128, 256)
        for half in range(2):
            flat_ref[half, pl.ds(pl.multiple_of(i * 128, 128), 128), :] = values[
                :, half * 128 : (half + 1) * 128
            ]
        return carry

    lax.fori_loop(0, 8, load, 0)

    def step(g, carry):
        windows = []
        for b in range(16):
            at = pl.ds(b, 64, stride=16)
            windows.append(
                jnp.concatenate([flat_ref[half, at, :] for half in range(2)], axis=1)
            )
        out = attend_and_mix(jnp.concatenate(windows, axis=0), w)
        for b in range(16):
            at = pl.ds(b, 64, stride=16)
            for half in range(2):
                flat_ref[half, at, :] = out[
                    b * 64 : (b + 1) * 64, half * 128 : (half + 1) * 128
                ]
        return carry

    step(0, 0)

    def store(i, carry):
        at = pl.ds(pl.multiple_of(i * 128, 128), 128)
        values = jnp.concatenate([flat_ref[half, at, :] for half in range(2)], axis=1)
        out_ref[pl.ds(i * 8, 8)] = values.astype(BF16).reshape(8, 16, 256)
        return carry

    lax.fori_loop(0, 8, store, 0)


def block_section(k, own, up, down, weights):
    return pl.pallas_call(
        functools.partial(block_kernel, k),
        out_shape=jax.ShapeDtypeStruct((8, 8, 16, 256), BF16),
        compiler_params=pltpu.CompilerParams(vmem_limit_bytes=VMEM_LIMIT),
        name="block_section",
    )(own, up, down, *weights)


def grid_section(x, weights):
    return pl.pallas_call(
        grid_kernel,
        out_shape=jax.ShapeDtypeStruct((64, 16, 256), BF16),
        scratch_shapes=[pltpu.VMEM((2, 1024, 128), F32)],
        compiler_params=pltpu.CompilerParams(vmem_limit_bytes=VMEM_LIMIT),
        name="grid_section",
    )(x, *weights)


def body(
    stem_strips, norm_scale, norm_shift, expand_weight, depth_weight, project_weight,
    block_gain, block_inputs, block_output, block_bias, first_gain, first_up, first_down,
    grid_gain, grid_inputs, grid_output, grid_bias, second_gain, second_up, second_down,
):
    row = lambda a: a.reshape(1, -1)
    both = ("rows", "cols")
    top = lax.ppermute(stem_strips[5:6], both, [(d, d + 1) for d in range(127)])
    bot = lax.ppermute(stem_strips[0:1], both, [(d + 1, d) for d in range(127)])
    own, up, down = bottleneck(
        stem_strips, top, bot, row(norm_scale), row(norm_shift), expand_weight,
        depth_weight, project_weight,
    )
    up = lax.ppermute(up, "cols", Y_UP)
    down = lax.ppermute(down, "cols", Y_DOWN)
    block_weights = (
        row(block_gain), block_inputs, block_output, block_bias,
        row(first_gain), first_up, first_down,
    )
    grid_weights = (
        row(grid_gain), grid_inputs, grid_output, grid_bias,
        row(second_gain), second_up, second_down,
    )
    done = [block_section(k, own, up, down, block_weights) for k in range(3)]
    sent = jnp.stack(done, axis=1)
    arrived = lax.all_to_all(sent, "rows", 0, 0, axis_index_groups=CORE_ROWS, tiled=True)
    grids = [grid_section(arrived[:, k], grid_weights) for k in range(3)]
    back = jnp.stack(grids, axis=1)
    landed = lax.all_to_all(back, both, 0, 0, axis_index_groups=CORE_ALL, tiled=True)
    landed = landed.reshape(8, 2, 3, 4, 16, 256).transpose(1, 2, 0, 3, 4, 5)
    return landed.reshape(48, 64, 256)


def solution(mesh):
    return jax.shard_map(
        body,
        mesh=mesh,
        in_specs=(P(("rows", "cols"), None, None),) + (P(),) * 19,
        out_specs=P("rows", "cols", None),
        check_vma=False,
    )
```

```python
import functools

import jax
import jax.numpy as jnp
from jax import lax
from jax.experimental import pallas as pl
from jax.experimental.pallas import tpu as pltpu
from jax.sharding import PartitionSpec as P

EPSILON = 1e-05
LOG2E = 1.4426950408889634
GELU_A = 0.7978845608028654
GELU_B = GELU_A * 0.044715
F32 = jnp.float32
BF16 = jnp.bfloat16

CORE_ROWS = [[core + 2 * i for i in range(8)] for core in range(2)]
CORE_ALL = [[(core + 2 * i) * 8 + c for i in range(8) for c in range(8)] for core in range(2)]
Y_UP = [(c, c + 1) for c in range(7) if c % 4 != 3]
Y_DOWN = [(c + 1, c) for c in range(7) if c % 4 != 3]


def twice_gelu(x):
    inner = x * (GELU_B * (x * x) + GELU_A)
    return x * (1.0 + jnp.tanh(inner))


def own_y():
    return lax.rem(lax.axis_index("cols"), 4)


PAD = 8


def twice_gelu_short(x):
    x = x.astype(BF16)
    inner = x * (BF16(GELU_B) * (x * x) + BF16(GELU_A))
    return x * (BF16(1.0) + jnp.tanh(inner))


def clear_edges(e_ref):
    edge = jnp.zeros((PAD, 128), F32)

    def clear(index, carry):
        for lb in range(8):
            e_ref[index, lb, 0:PAD, :] = edge
            e_ref[index, lb, 512 + PAD : 512 + 2 * PAD, :] = edge
        return carry

    lax.fori_loop(0, e_ref.shape[0], clear, 0)


def expand_row(values, scale, shift, we_ref, e_ref, row, factor):
    normed = (values.astype(F32) * scale + shift).astype(BF16)
    for nb in range(4):
        flat = jnp.dot(normed, we_ref[:, nb * 256 : (nb + 1) * 256], preferred_element_type=F32)
        wide = twice_gelu(flat)
        if factor is not None:
            wide = wide * factor
        for half in range(2):
            e_ref[row, nb * 2 + half, PAD : 512 + PAD, :] = wide[:, half * 128 : (half + 1) * 128]


def depth_row(sources, x_ref, row, taps, wp_ref, out_ref, at_row):
    for side in range(2):
        base = side * 256
        total = jnp.zeros((256, 256), F32)
        for pair in range(4):
            parts = []
            for lb in (2 * pair, 2 * pair + 1):
                acc = None
                for tap in range(9):
                    e_ref, at = sources[tap // 3]
                    term = (
                        e_ref[at, lb, pl.ds(base + PAD - 1 + tap % 3, 256), :]
                        * taps[tap : tap + 1, lb * 128 : (lb + 1) * 128]
                    )
                    acc = term if acc is None else acc + term
                parts.append(twice_gelu_short(acc))
            wide = jnp.concatenate(parts, axis=1)
            total = total + jnp.dot(
                wide, wp_ref[pair * 256 : (pair + 1) * 256, :], preferred_element_type=F32
            )
        values = x_ref[row, base : base + 256, :].astype(F32)
        result = (values + 0.5 * total).astype(BF16)
        for jj in range(4):
            for tp in range(4):
                at = jj * 64 + tp * 16
                out_ref[at_row * 4 + tp, 4 * side + jj] = result[at : at + 16]


def middle_kernel(
    x_hbm, scale_hbm, shift_hbm, we_hbm, dw_hbm, wp_hbm, mid_ref, e_ref,
    x_ref, scale_ref, shift_ref, we_ref, dw_ref, wp_ref, sem,
):
    pairs = [(scale_hbm, scale_ref), (shift_hbm, shift_ref), (we_hbm, we_ref)]
    pairs += [(x_hbm.at[r], x_ref.at[r]) for r in range(6)]
    pairs += [(dw_hbm, dw_ref), (wp_hbm, wp_ref)]
    copies = [pltpu.make_async_copy(a, b, sem.at[n]) for n, (a, b) in enumerate(pairs)]
    for copy in copies:
        copy.start()
    clear_edges(e_ref)
    for copy in copies[:3]:
        copy.wait()
    scale, shift = scale_ref[...], shift_ref[...]
    for row in range(6):
        copies[3 + row].wait()
        expand_row(x_ref[row], scale, shift, we_ref, e_ref, row, None)
    for copy in copies[9:]:
        copy.wait()
    taps = dw_ref[...] * 0.5

    def depth(step, carry):
        for row in (2 * step + 1, 2 * step + 2):
            sources = [(e_ref, row - 1), (e_ref, row), (e_ref, row + 1)]
            depth_row(sources, x_ref, row, taps, wp_ref, mid_ref, row - 1)
        return carry

    lax.fori_loop(0, 2, depth, 0)


def edge_kernel(
    x_ref, top_ref, bot_ref, e_ref, mid_ref, scale_ref, shift_ref, we_ref, dw_ref, wp_ref,
    edge_ref, up_l_ref, down_l_ref, up_r_ref, down_r_ref, halo_ref,
):
    device = lax.axis_index("rows") * 8 + lax.axis_index("cols")
    scale, shift = scale_ref[...], shift_ref[...]
    clear_edges(halo_ref)
    expand_row(top_ref[0], scale, shift, we_ref, halo_ref, 0, (device > 0).astype(F32))
    expand_row(bot_ref[0], scale, shift, we_ref, halo_ref, 1, (device < 127).astype(F32))
    taps = dw_ref[...] * 0.5
    sources = [(halo_ref, 0), (e_ref, 0), (e_ref, 1)]
    depth_row(sources, x_ref, 0, taps, wp_ref, edge_ref, 0)
    sources = [(e_ref, 4), (e_ref, 5), (halo_ref, 1)]
    depth_row(sources, x_ref, 5, taps, wp_ref, edge_ref, 1)
    v = own_y()

    def send(row, tp, m, left_ref, right_ref):
        inside = jnp.logical_and(row >= 1, row <= 4)

        @pl.when(inside)
        def _():
            at = jnp.clip(row - 1, 0, 3) * 4 + tp
            left_ref[m] = mid_ref[at, 0:4]
            right_ref[m] = mid_ref[at, 4:8]

        @pl.when(jnp.logical_not(inside))
        def _():
            at = jnp.where(row == 5, 4, 0) + tp
            left_ref[m] = edge_ref[at, 0:4]
            right_ref[m] = edge_ref[at, 4:8]

    def pick(m, carry):
        n_up = v + 1
        tp = jnp.clip(3 - v + lax.rem(m, n_up), 0, 3)
        send(jnp.minimum(2 * v + m // n_up, 5), tp, m, up_l_ref, up_r_ref)
        n_down = 4 - v
        send(jnp.minimum(m // n_down, 5), lax.rem(m, n_down), m, down_l_ref, down_r_ref)
        return carry

    lax.fori_loop(0, 8, pick, 0)


def vmem(limit):
    return pltpu.CompilerParams(vmem_limit_bytes=limit * 1024 * 1024)


def pieces(count, columns):
    return jax.ShapeDtypeStruct((count, columns, 16, 256), BF16)


def bottleneck_middle(strips, scale, shift, we, dw, wp):
    return pl.pallas_call(
        middle_kernel,
        out_shape=[pieces(16, 8), jax.ShapeDtypeStruct((6, 8, 512 + 2 * PAD, 128), F32)],
        in_specs=[pl.BlockSpec(memory_space=pltpu.HBM)] * 6,
        scratch_shapes=[
            pltpu.VMEM((6, 512, 256), BF16),
            pltpu.VMEM((1, 256), F32),
            pltpu.VMEM((1, 256), F32),
            pltpu.VMEM((256, 1024), BF16),
            pltpu.VMEM((9, 1024), F32),
            pltpu.VMEM((1024, 256), BF16),
            pltpu.SemaphoreType.DMA((11,)),
        ],
        compiler_params=vmem(24),
        name="bottleneck_middle",
    )(strips, scale, shift, we, dw, wp)


def bottleneck_edge(strips, top, bot, expanded, middle, scale, shift, we, dw, wp):
    return pl.pallas_call(
        edge_kernel,
        out_shape=[pieces(8, 8)] + [pieces(8, 4)] * 4,
        scratch_shapes=[pltpu.VMEM((2, 8, 512 + 2 * PAD, 128), F32)],
        compiler_params=vmem(24),
        name="bottleneck_edge",
    )(strips, top, bot, expanded, middle, scale, shift, we, dw, wp)


def normed_of(x, gain):
    center = x - jnp.mean(x, axis=-1, keepdims=True)
    spread = jnp.mean(center * center, axis=-1, keepdims=True)
    return (center * lax.rsqrt(spread + EPSILON) * gain).astype(BF16)


def head_masks(dtype):
    lane = lax.broadcasted_iota(jnp.int32, (1, 128), 1)
    return [(lane // 32 == h).astype(F32).astype(dtype) for h in range(4)]


def attend_and_mix(x, w):
    tokens = x.shape[0]
    masks = head_masks(BF16)
    key_head = lax.broadcasted_iota(jnp.int32, (256, 128), 0) // 64
    lane_head = lax.broadcasted_iota(jnp.int32, (256, 128), 1) // 32
    head_ones = (key_head == lane_head).astype(F32).astype(BF16)
    score_lane = lax.broadcasted_iota(jnp.int32, (64, 256), 1)
    bias = [
        jnp.concatenate([w["bias"][4 * g + h] for h in range(4)], axis=1) * LOG2E
        for g in range(2)
    ]
    normed = normed_of(x, w["gain_a"][...])
    q, k, v = [
        jnp.dot(normed, w["inputs"][:, c * 256 : (c + 1) * 256], preferred_element_type=F32).astype(
            BF16
        )
        for c in range(3)
    ]
    rows = []
    for win in range(tokens // 64):
        at = slice(win * 64, (win + 1) * 64)
        groups = []
        for g in range(2):
            lanes = slice(g * 128, (g + 1) * 128)
            qg, kg, vg = q[at, lanes], k[at, lanes], v[at, lanes]
            keys = jnp.concatenate([kg * masks[h] for h in range(4)], axis=0)
            values = jnp.concatenate([vg * masks[h] for h in range(4)], axis=0)
            values = jnp.concatenate([values, head_ones], axis=1)
            scores = lax.dot_general(
                qg, keys, (((1,), (1,)), ((), ())), preferred_element_type=F32
            )
            scores = scores * (LOG2E * 32**-0.5) + bias[g]
            top = None
            for h in range(4):
                peak = jnp.max(scores[:, h * 64 : (h + 1) * 64], axis=1, keepdims=True)
                top = (
                    jnp.broadcast_to(peak, (64, 256))
                    if top is None
                    else jnp.where(score_lane >= h * 64, peak, top)
                )
            weights = jnp.exp2(scores - top).astype(BF16)
            mixed = jnp.dot(weights, values, preferred_element_type=F32)
            groups.append((mixed[:, :128] * (1.0 / mixed[:, 128:])).astype(BF16))
        rows.append(jnp.concatenate(groups, axis=1))
    combined = jnp.concatenate(rows, axis=0)
    x = x + jnp.dot(combined, w["output"][...], preferred_element_type=F32)
    x = x.astype(BF16).astype(F32)
    normed = normed_of(x, w["gain_m"][...])
    total = jnp.zeros((tokens, 256), F32)
    for c in range(4):
        cols = slice(c * 256, (c + 1) * 256)
        hidden = jnp.dot(normed, w["up"][:, cols], preferred_element_type=F32)
        hidden = twice_gelu(hidden).astype(BF16)
        total = total + jnp.dot(hidden, w["down"][cols, :], preferred_element_type=F32)
    return x + 0.5 * total


NAMES = ("gain_a", "inputs", "output", "bias", "gain_m", "up", "down")


def block_places():
    y = own_y()
    places = []
    for k in range(3):
        n = 3 * y + k
        p = n // 4
        tp = lax.rem(n, 4)
        for s in range(8):
            row = 8 * p + s
            owner = row // 6
            local = row - 6 * owner
            v = jnp.maximum(y - 1, 0)
            m_up = jnp.clip((local - 2 * v) * (v + 1) + tp - (3 - v), 0, 7)
            v = jnp.minimum(y + 1, 3)
            m_down = jnp.clip(local * (4 - v) + tp, 0, 7)
            inside = jnp.logical_and(local >= 1, local <= 4)
            at_mid = jnp.clip(local - 1, 0, 3) * 4 + tp
            at_edge = jnp.where(local == 5, 4, 0) + tp
            places.append((owner, inside, at_mid, at_edge, m_up, m_down))
    return y, places


def block_kernel(half, mid_ref, edge_ref, up_ref, down_ref, *refs):
    w = dict(zip(NAMES, refs))
    refs = refs[len(NAMES) :]
    if half == 1:
        done_ref, out_ref = refs
        out_ref[:, :, 0:4] = done_ref[...]
    else:
        (out_ref,) = refs
    y, places = block_places()
    units = []
    js = slice(4 * half, 4 * half + 4)
    for owner, inside, at_mid, at_edge, m_up, m_down in places:
        mine = jnp.where(inside, mid_ref[at_mid, js].astype(F32), edge_ref[at_edge, js].astype(F32))
        above = up_ref[m_up].astype(F32)
        below = down_ref[m_down].astype(F32)
        units.append(jnp.where(owner == y, mine, jnp.where(owner < y, above, below)))
    windows = [(k, jj, t) for k in range(3) for jj in range(4) for t in range(2)]
    x = jnp.concatenate(
        [units[k * 8 + s][jj, t * 8 : (t + 1) * 8, :] for k, jj, t in windows for s in range(8)],
        axis=0,
    )
    out = attend_and_mix(x, w)
    for k in range(3):
        for jj in range(4):
            first = (k * 4 + jj) * 128
            for s in range(8):
                both = [out[first + t * 64 + s * 8 :][:8] for t in range(2)]
                out_ref[s, k, jj + 4 * half] = jnp.concatenate(both, axis=0).astype(BF16)


def grid_kernel(x_ref, *refs):
    w = dict(zip(NAMES, refs))
    out_ref, flat_ref = refs[len(NAMES) :]

    def slot(k, carry):
        for i in range(8):
            values = x_ref[i, k].astype(F32).reshape(128, 256)
            for half in range(2):
                flat_ref[half, i * 128 : (i + 1) * 128, :] = values[
                    :, half * 128 : (half + 1) * 128
                ]
        windows = []
        for b in range(16):
            at = pl.ds(b, 64, stride=16)
            windows.append(
                jnp.concatenate([flat_ref[half, at, :] for half in range(2)], axis=1)
            )
        out = attend_and_mix(jnp.concatenate(windows, axis=0), w)
        for b in range(16):
            at = pl.ds(b, 64, stride=16)
            for half in range(2):
                flat_ref[half, at, :] = out[
                    b * 64 : (b + 1) * 64, half * 128 : (half + 1) * 128
                ]
        for i in range(8):
            values = jnp.concatenate(
                [flat_ref[half, i * 128 : (i + 1) * 128, :] for half in range(2)], axis=1
            )
            out_ref[pl.ds(i * 8, 8), k] = values.astype(BF16).reshape(8, 16, 256)
        return carry

    lax.fori_loop(0, 3, slot, 0)


def block_section(half, mid, edge, up, down, weights, *done):
    return pl.pallas_call(
        functools.partial(block_kernel, half),
        out_shape=jax.ShapeDtypeStruct((8, 3, 4 if half == 0 else 8, 16, 256), BF16),
        compiler_params=vmem(24),
        name="block_section",
    )(mid, edge, up, down, *weights, *done)


def grid_section(x, weights):
    return pl.pallas_call(
        grid_kernel,
        out_shape=jax.ShapeDtypeStruct((64, 3, 16, 256), BF16),
        scratch_shapes=[pltpu.VMEM((2, 1024, 128), F32)],
        compiler_params=vmem(24),
        name="grid_section",
    )(x, *weights)


def body(
    stem_strips, norm_scale, norm_shift, expand_weight, depth_weight, project_weight,
    block_gain, block_inputs, block_output, block_bias, first_gain, first_up, first_down,
    grid_gain, grid_inputs, grid_output, grid_bias, second_gain, second_up, second_down,
):
    row = lambda a: a.reshape(1, -1)
    both = ("rows", "cols")
    top = lax.ppermute(stem_strips[5:6], both, [(d, d + 1) for d in range(127)])
    bot = lax.ppermute(stem_strips[0:1], both, [(d + 1, d) for d in range(127)])
    weights = (row(norm_scale), row(norm_shift), expand_weight, depth_weight, project_weight)
    middle, expanded = bottleneck_middle(
        *[pltpu.with_memory_space_constraint(a, pltpu.HBM) for a in (stem_strips, *weights)]
    )
    edge, up_l, down_l, up_r, down_r = bottleneck_edge(
        stem_strips, top, bot, expanded, middle, *weights
    )
    up_l, up_r = [lax.ppermute(a, "cols", Y_UP) for a in (up_l, up_r)]
    down_l, down_r = [lax.ppermute(a, "cols", Y_DOWN) for a in (down_l, down_r)]
    block_weights = (
        row(block_gain), block_inputs, block_output, block_bias,
        row(first_gain), first_up, first_down,
    )
    grid_weights = (
        row(grid_gain), grid_inputs, grid_output, grid_bias,
        row(second_gain), second_up, second_down,
    )
    left = block_section(0, middle, edge, up_l, down_l, block_weights)
    sent = block_section(1, middle, edge, up_r, down_r, block_weights, left)
    arrived = lax.all_to_all(sent, "rows", 0, 0, axis_index_groups=CORE_ROWS, tiled=True)
    back = grid_section(arrived, grid_weights)
    landed = lax.all_to_all(back, both, 0, 0, axis_index_groups=CORE_ALL, tiled=True)
    landed = landed.reshape(8, 2, 3, 4, 16, 256).transpose(1, 2, 0, 3, 4, 5)
    return landed.reshape(48, 64, 256)


def solution(mesh):
    return jax.shard_map(
        body,
        mesh=mesh,
        in_specs=(P(("rows", "cols"), None, None),) + (P(),) * 19,
        out_specs=P("rows", "cols", None),
        check_vma=False,
    )
```

```python
import functools

import jax
import jax.numpy as jnp
from jax import lax
from jax.experimental import pallas as pl
from jax.experimental.pallas import tpu as pltpu
from jax.sharding import PartitionSpec as P

EPSILON = 1e-05
LOG2E = 1.4426950408889634
GELU_A = 0.7978845608028654
GELU_B = GELU_A * 0.044715
F32 = jnp.float32
BF16 = jnp.bfloat16

CORE_ROWS = [[core + 2 * i for i in range(8)] for core in range(2)]
CORE_ALL = [[(core + 2 * i) * 8 + c for i in range(8) for c in range(8)] for core in range(2)]
Y_UP = [(c, c // 4 * 4 + (c + 1) % 4) for c in range(8)]
Y_DOWN = [(b, a) for a, b in Y_UP]
STRIP_DOWN = [(d, (d + 1) % 128) for d in range(128)]
STRIP_UP = [(b, a) for a, b in STRIP_DOWN]


def twice_gelu(x):
    inner = x * (GELU_B * (x * x) + GELU_A)
    return x * (1.0 + jnp.tanh(inner))


def own_y():
    return lax.rem(lax.axis_index("cols"), 4)


PAD = 8


def twice_gelu_short(x):
    x = x.astype(BF16)
    inner = x * (BF16(GELU_B) * (x * x) + BF16(GELU_A))
    return x * (BF16(1.0) + jnp.tanh(inner))


def clear_edges(e_ref):
    edge = jnp.zeros((PAD, 128), F32)

    def clear(index, carry):
        for lb in range(8):
            e_ref[index, lb, 0:PAD, :] = edge
            e_ref[index, lb, 512 + PAD : 512 + 2 * PAD, :] = edge
        return carry

    lax.fori_loop(0, e_ref.shape[0], clear, 0)


def expand_row(values, scale, shift, we_ref, e_ref, row, factor):
    normed = (values.astype(F32) * scale + shift).astype(BF16)
    for nb in range(4):
        flat = jnp.dot(normed, we_ref[:, nb * 256 : (nb + 1) * 256], preferred_element_type=F32)
        wide = twice_gelu(flat)
        if factor is not None:
            wide = wide * factor
        for half in range(2):
            e_ref[row, nb * 2 + half, PAD : 512 + PAD, :] = wide[:, half * 128 : (half + 1) * 128]


def depth_row(sources, x_ref, row, taps, wp_ref, out_ref, at_row):
    for side in range(2):
        base = side * 256
        total = jnp.zeros((256, 256), F32)
        for pair in range(4):
            parts = []
            for lb in (2 * pair, 2 * pair + 1):
                acc = None
                for tap in range(9):
                    e_ref, at = sources[tap // 3]
                    term = (
                        e_ref[at, lb, pl.ds(base + PAD - 1 + tap % 3, 256), :]
                        * taps[tap : tap + 1, lb * 128 : (lb + 1) * 128]
                    )
                    acc = term if acc is None else acc + term
                parts.append(twice_gelu_short(acc))
            wide = jnp.concatenate(parts, axis=1)
            total = total + jnp.dot(
                wide, wp_ref[pair * 256 : (pair + 1) * 256, :], preferred_element_type=F32
            )
        values = x_ref[row, base : base + 256, :].astype(F32)
        result = (values + 0.5 * total).astype(BF16)
        for jj in range(4):
            for tp in range(4):
                at = jj * 64 + tp * 16
                out_ref[at_row * 4 + tp, 4 * side + jj] = result[at : at + 16]


def middle_kernel(
    x_hbm, scale_hbm, shift_hbm, we_hbm, dw_hbm, wp_hbm, mid_ref, e_ref,
    x_ref, scale_ref, shift_ref, we_ref, dw_ref, wp_ref, sem,
):
    pairs = [(scale_hbm, scale_ref), (shift_hbm, shift_ref), (we_hbm, we_ref)]
    pairs += [(x_hbm.at[r], x_ref.at[r]) for r in range(6)]
    pairs += [(dw_hbm, dw_ref), (wp_hbm, wp_ref)]
    copies = [pltpu.make_async_copy(a, b, sem.at[n]) for n, (a, b) in enumerate(pairs)]
    for copy in copies:
        copy.start()
    clear_edges(e_ref)
    for copy in copies[:3]:
        copy.wait()
    scale, shift = scale_ref[...], shift_ref[...]
    for row in range(6):
        copies[3 + row].wait()
        expand_row(x_ref[row], scale, shift, we_ref, e_ref, row, None)
    for copy in copies[9:]:
        copy.wait()
    taps = dw_ref[...] * 0.5

    def depth(step, carry):
        for row in (2 * step + 1, 2 * step + 2):
            sources = [(e_ref, row - 1), (e_ref, row), (e_ref, row + 1)]
            depth_row(sources, x_ref, row, taps, wp_ref, mid_ref, row - 1)
        return carry

    lax.fori_loop(0, 2, depth, 0)


def edge_kernel(
    x_ref, top_ref, bot_ref, e_ref, mid_ref, scale_ref, shift_ref, we_ref, dw_ref, wp_ref,
    edge_ref, up_l_ref, down_l_ref, up_r_ref, down_r_ref, halo_ref,
):
    device = lax.axis_index("rows") * 8 + lax.axis_index("cols")
    scale, shift = scale_ref[...], shift_ref[...]
    clear_edges(halo_ref)
    expand_row(top_ref[0], scale, shift, we_ref, halo_ref, 0, (device > 0).astype(F32))
    expand_row(bot_ref[0], scale, shift, we_ref, halo_ref, 1, (device < 127).astype(F32))
    taps = dw_ref[...] * 0.5
    sources = [(halo_ref, 0), (e_ref, 0), (e_ref, 1)]
    depth_row(sources, x_ref, 0, taps, wp_ref, edge_ref, 0)
    sources = [(e_ref, 4), (e_ref, 5), (halo_ref, 1)]
    depth_row(sources, x_ref, 5, taps, wp_ref, edge_ref, 1)
    v = own_y()

    def send(row, tp, m, left_ref, right_ref):
        inside = jnp.logical_and(row >= 1, row <= 4)

        @pl.when(inside)
        def _():
            at = jnp.clip(row - 1, 0, 3) * 4 + tp
            left_ref[m] = mid_ref[at, 0:4]
            right_ref[m] = mid_ref[at, 4:8]

        @pl.when(jnp.logical_not(inside))
        def _():
            at = jnp.where(row == 5, 4, 0) + tp
            left_ref[m] = edge_ref[at, 0:4]
            right_ref[m] = edge_ref[at, 4:8]

    def pick(m, carry):
        n_up = v + 1
        tp = jnp.clip(3 - v + lax.rem(m, n_up), 0, 3)
        send(jnp.minimum(2 * v + m // n_up, 5), tp, m, up_l_ref, up_r_ref)
        n_down = 4 - v
        send(jnp.minimum(m // n_down, 5), lax.rem(m, n_down), m, down_l_ref, down_r_ref)
        return carry

    lax.fori_loop(0, 8, pick, 0)


def vmem(limit):
    return pltpu.CompilerParams(vmem_limit_bytes=limit * 1024 * 1024)


def pieces(count, columns):
    return jax.ShapeDtypeStruct((count, columns, 16, 256), BF16)


def bottleneck_middle(strips, scale, shift, we, dw, wp):
    return pl.pallas_call(
        middle_kernel,
        out_shape=[pieces(16, 8), jax.ShapeDtypeStruct((6, 8, 512 + 2 * PAD, 128), F32)],
        in_specs=[pl.BlockSpec(memory_space=pltpu.HBM)] * 6,
        scratch_shapes=[
            pltpu.VMEM((6, 512, 256), BF16),
            pltpu.VMEM((1, 256), F32),
            pltpu.VMEM((1, 256), F32),
            pltpu.VMEM((256, 1024), BF16),
            pltpu.VMEM((9, 1024), F32),
            pltpu.VMEM((1024, 256), BF16),
            pltpu.SemaphoreType.DMA((11,)),
        ],
        compiler_params=vmem(24),
        name="bottleneck_middle",
    )(strips, scale, shift, we, dw, wp)


def bottleneck_edge(strips, top, bot, expanded, middle, scale, shift, we, dw, wp):
    return pl.pallas_call(
        edge_kernel,
        out_shape=[pieces(8, 8)] + [pieces(8, 4)] * 4,
        scratch_shapes=[pltpu.VMEM((2, 8, 512 + 2 * PAD, 128), F32)],
        compiler_params=vmem(24),
        name="bottleneck_edge",
    )(strips, top, bot, expanded, middle, scale, shift, we, dw, wp)


def normed_of(x, gain):
    center = x - jnp.mean(x, axis=-1, keepdims=True)
    spread = jnp.mean(center * center, axis=-1, keepdims=True)
    return (center * lax.rsqrt(spread + EPSILON) * gain).astype(BF16)


def head_masks(dtype):
    lane = lax.broadcasted_iota(jnp.int32, (1, 128), 1)
    return [(lane // 32 == h).astype(F32).astype(dtype) for h in range(4)]


def attend_and_mix(x, w):
    tokens = x.shape[0]
    masks = head_masks(BF16)
    key_head = lax.broadcasted_iota(jnp.int32, (256, 128), 0) // 64
    lane_head = lax.broadcasted_iota(jnp.int32, (256, 128), 1) // 32
    head_ones = (key_head == lane_head).astype(F32).astype(BF16)
    score_lane = lax.broadcasted_iota(jnp.int32, (64, 256), 1)
    bias = [
        jnp.concatenate([w["bias"][4 * g + h] for h in range(4)], axis=1) * LOG2E
        for g in range(2)
    ]
    normed = normed_of(x, w["gain_a"][...])
    q, k, v = [
        jnp.dot(normed, w["inputs"][:, c * 256 : (c + 1) * 256], preferred_element_type=F32).astype(
            BF16
        )
        for c in range(3)
    ]
    rows = []
    for win in range(tokens // 64):
        at = slice(win * 64, (win + 1) * 64)
        groups = []
        for g in range(2):
            lanes = slice(g * 128, (g + 1) * 128)
            qg, kg, vg = q[at, lanes], k[at, lanes], v[at, lanes]
            keys = jnp.concatenate([kg * masks[h] for h in range(4)], axis=0)
            values = jnp.concatenate([vg * masks[h] for h in range(4)], axis=0)
            values = jnp.concatenate([values, head_ones], axis=1)
            scores = lax.dot_general(
                qg, keys, (((1,), (1,)), ((), ())), preferred_element_type=F32
            )
            scores = scores * (LOG2E * 32**-0.5) + bias[g]
            top = None
            for h in range(4):
                peak = jnp.max(scores[:, h * 64 : (h + 1) * 64], axis=1, keepdims=True)
                top = (
                    jnp.broadcast_to(peak, (64, 256))
                    if top is None
                    else jnp.where(score_lane >= h * 64, peak, top)
                )
            weights = jnp.exp2(scores - top).astype(BF16)
            mixed = jnp.dot(weights, values, preferred_element_type=F32)
            groups.append((mixed[:, :128] * (1.0 / mixed[:, 128:])).astype(BF16))
        rows.append(jnp.concatenate(groups, axis=1))
    combined = jnp.concatenate(rows, axis=0)
    x = x + jnp.dot(combined, w["output"][...], preferred_element_type=F32)
    x = x.astype(BF16).astype(F32)
    normed = normed_of(x, w["gain_m"][...])
    total = jnp.zeros((tokens, 256), F32)
    for c in range(4):
        cols = slice(c * 256, (c + 1) * 256)
        hidden = jnp.dot(normed, w["up"][:, cols], preferred_element_type=F32)
        hidden = twice_gelu(hidden).astype(BF16)
        total = total + jnp.dot(hidden, w["down"][cols, :], preferred_element_type=F32)
    return x + 0.5 * total


NAMES = ("gain_a", "inputs", "output", "bias", "gain_m", "up", "down")


def block_places():
    y = own_y()
    places = []
    for k in range(3):
        n = 3 * y + k
        p = n // 4
        tp = lax.rem(n, 4)
        for s in range(8):
            row = 8 * p + s
            owner = row // 6
            local = row - 6 * owner
            v = jnp.maximum(y - 1, 0)
            m_up = jnp.clip((local - 2 * v) * (v + 1) + tp - (3 - v), 0, 7)
            v = jnp.minimum(y + 1, 3)
            m_down = jnp.clip(local * (4 - v) + tp, 0, 7)
            inside = jnp.logical_and(local >= 1, local <= 4)
            at_mid = jnp.clip(local - 1, 0, 3) * 4 + tp
            at_edge = jnp.where(local == 5, 4, 0) + tp
            places.append((owner, inside, at_mid, at_edge, m_up, m_down))
    return y, places


def block_kernel(half, mid_ref, edge_ref, up_ref, down_ref, *refs):
    w = dict(zip(NAMES, refs))
    refs = refs[len(NAMES) :]
    if half == 1:
        done_ref, out_ref = refs
        out_ref[:, :, 0:4] = done_ref[...]
    else:
        (out_ref,) = refs
    y, places = block_places()
    units = []
    js = slice(4 * half, 4 * half + 4)
    for owner, inside, at_mid, at_edge, m_up, m_down in places:
        mine = jnp.where(inside, mid_ref[at_mid, js].astype(F32), edge_ref[at_edge, js].astype(F32))
        above = up_ref[m_up].astype(F32)
        below = down_ref[m_down].astype(F32)
        units.append(jnp.where(owner == y, mine, jnp.where(owner < y, above, below)))
    windows = [(k, jj, t) for k in range(3) for jj in range(4) for t in range(2)]
    x = jnp.concatenate(
        [units[k * 8 + s][jj, t * 8 : (t + 1) * 8, :] for k, jj, t in windows for s in range(8)],
        axis=0,
    )
    out = attend_and_mix(x, w)
    for k in range(3):
        for jj in range(4):
            first = (k * 4 + jj) * 128
            for s in range(8):
                both = [out[first + t * 64 + s * 8 :][:8] for t in range(2)]
                out_ref[s, k, jj + 4 * half] = jnp.concatenate(both, axis=0).astype(BF16)


def grid_kernel(x_ref, *refs):
    w = dict(zip(NAMES, refs))
    out_ref, flat_ref = refs[len(NAMES) :]

    def slot(k, carry):
        for i in range(8):
            values = x_ref[i, k].astype(F32).reshape(128, 256)
            for half in range(2):
                flat_ref[half, i * 128 : (i + 1) * 128, :] = values[
                    :, half * 128 : (half + 1) * 128
                ]
        windows = []
        for b in range(16):
            at = pl.ds(b, 64, stride=16)
            windows.append(
                jnp.concatenate([flat_ref[half, at, :] for half in range(2)], axis=1)
            )
        out = attend_and_mix(jnp.concatenate(windows, axis=0), w)
        for b in range(16):
            at = pl.ds(b, 64, stride=16)
            for half in range(2):
                flat_ref[half, at, :] = out[
                    b * 64 : (b + 1) * 64, half * 128 : (half + 1) * 128
                ]
        for i in range(8):
            values = jnp.concatenate(
                [flat_ref[half, i * 128 : (i + 1) * 128, :] for half in range(2)], axis=1
            )
            out_ref[pl.ds(i * 8, 8), k] = values.astype(BF16).reshape(8, 16, 256)
        return carry

    lax.fori_loop(0, 3, slot, 0)


def block_section(half, mid, edge, up, down, weights, *done):
    return pl.pallas_call(
        functools.partial(block_kernel, half),
        out_shape=jax.ShapeDtypeStruct((8, 3, 4 if half == 0 else 8, 16, 256), BF16),
        compiler_params=vmem(24),
        name="block_section",
    )(mid, edge, up, down, *weights, *done)


def grid_section(x, weights):
    return pl.pallas_call(
        grid_kernel,
        out_shape=jax.ShapeDtypeStruct((64, 3, 16, 256), BF16),
        scratch_shapes=[pltpu.VMEM((2, 1024, 128), F32)],
        compiler_params=vmem(24),
        name="grid_section",
    )(x, *weights)


def body(
    stem_strips, norm_scale, norm_shift, expand_weight, depth_weight, project_weight,
    block_gain, block_inputs, block_output, block_bias, first_gain, first_up, first_down,
    grid_gain, grid_inputs, grid_output, grid_bias, second_gain, second_up, second_down,
):
    row = lambda a: a.reshape(1, -1)
    both = ("rows", "cols")
    top = lax.ppermute(stem_strips[5:6], both, STRIP_DOWN)
    bot = lax.ppermute(stem_strips[0:1], both, STRIP_UP)
    weights = (row(norm_scale), row(norm_shift), expand_weight, depth_weight, project_weight)
    middle, expanded = bottleneck_middle(
        *[pltpu.with_memory_space_constraint(a, pltpu.HBM) for a in (stem_strips, *weights)]
    )
    edge, up_l, down_l, up_r, down_r = bottleneck_edge(
        stem_strips, top, bot, expanded, middle, *weights
    )
    up_l, up_r = [lax.ppermute(a, "cols", Y_UP) for a in (up_l, up_r)]
    down_l, down_r = [lax.ppermute(a, "cols", Y_DOWN) for a in (down_l, down_r)]
    block_weights = (
        row(block_gain), block_inputs, block_output, block_bias,
        row(first_gain), first_up, first_down,
    )
    grid_weights = (
        row(grid_gain), grid_inputs, grid_output, grid_bias,
        row(second_gain), second_up, second_down,
    )
    left = block_section(0, middle, edge, up_l, down_l, block_weights)
    sent = block_section(1, middle, edge, up_r, down_r, block_weights, left)
    arrived = lax.all_to_all(sent, "rows", 0, 0, axis_index_groups=CORE_ROWS, tiled=True)
    back = grid_section(arrived, grid_weights)
    landed = lax.all_to_all(back, both, 0, 0, axis_index_groups=CORE_ALL, tiled=True)
    landed = landed.reshape(8, 2, 3, 4, 16, 256).transpose(1, 2, 0, 3, 4, 5)
    return landed.reshape(48, 64, 256)


def solution(mesh):
    return jax.shard_map(
        body,
        mesh=mesh,
        in_specs=(P(("rows", "cols"), None, None),) + (P(),) * 19,
        out_specs=P("rows", "cols", None),
        check_vma=False,
    )
```

```python
import functools

import jax
import jax.numpy as jnp
from jax import lax
from jax.experimental import pallas as pl
from jax.experimental.pallas import tpu as pltpu
from jax.sharding import PartitionSpec as P

EPSILON = 1e-05
LOG2E = 1.4426950408889634
GELU_A = 0.7978845608028654
GELU_B = GELU_A * 0.044715
F32 = jnp.float32
BF16 = jnp.bfloat16

CORE_ROWS = [[core + 2 * i for i in range(8)] for core in range(2)]
CORE_ALL = [[(core + 2 * i) * 8 + c for i in range(8) for c in range(8)] for core in range(2)]
Y_UP = [(c, c // 4 * 4 + (c + 1) % 4) for c in range(8)]
Y_DOWN = [(b, a) for a, b in Y_UP]
STRIP_DOWN = [(d, (d + 1) % 128) for d in range(128)]
STRIP_UP = [(b, a) for a, b in STRIP_DOWN]


def twice_gelu(x):
    inner = x * (GELU_B * (x * x) + GELU_A)
    return x * (1.0 + jnp.tanh(inner))


def own_y():
    return lax.rem(lax.axis_index("cols"), 4)


PAD = 8
SPAN = 272
FIRST = (0, 240)


def twice_gelu_short(x):
    x = x.astype(BF16)
    inner = x * (BF16(GELU_B) * (x * x) + BF16(GELU_A))
    return x * (BF16(1.0) + jnp.tanh(inner))


def clear_edges(e_ref):
    edge = jnp.zeros((PAD, 128), F32)

    def clear(index, carry):
        for lb in range(8):
            e_ref[index, lb, 0:PAD, :] = edge
            e_ref[index, lb, SPAN + PAD : SPAN + 2 * PAD, :] = edge
        return carry

    lax.fori_loop(0, e_ref.shape[0], clear, 0)


def expand_row(values, scale, shift, we_ref, e_ref, row, factor):
    normed = (values.astype(F32) * scale + shift).astype(BF16)
    for nb in range(4):
        flat = jnp.dot(normed, we_ref[:, nb * 256 : (nb + 1) * 256], preferred_element_type=F32)
        wide = twice_gelu(flat)
        if factor is not None:
            wide = wide * factor
        for part in range(2):
            e_ref[row, nb * 2 + part, PAD : SPAN + PAD, :] = wide[:, part * 128 : (part + 1) * 128]


def depth_row(half, sources, values, taps, wp_ref, out_ref, at_row):
    base = 256 * half - FIRST[half] + PAD
    total = jnp.zeros((256, 256), F32)
    for pair in range(4):
        parts = []
        for lb in (2 * pair, 2 * pair + 1):
            acc = None
            for tap in range(9):
                e_ref, at = sources[tap // 3]
                term = (
                    e_ref[at, lb, pl.ds(base - 1 + tap % 3, 256), :]
                    * taps[tap : tap + 1, lb * 128 : (lb + 1) * 128]
                )
                acc = term if acc is None else acc + term
            parts.append(twice_gelu_short(acc))
        wide = jnp.concatenate(parts, axis=1)
        total = total + jnp.dot(
            wide, wp_ref[pair * 256 : (pair + 1) * 256, :], preferred_element_type=F32
        )
    result = (values.astype(F32) + 0.5 * total).astype(BF16)
    for jj in range(4):
        for tp in range(4):
            at = jj * 64 + tp * 16
            out_ref[at_row * 4 + tp, jj] = result[at : at + 16]


def middle_kernel(
    x_hbm, scale_hbm, shift_hbm, we_hbm, dw_hbm, wp_hbm, mid_ref, e_ref,
    x_ref, scale_ref, shift_ref, we_ref, dw_ref, wp_ref, sem,
):
    pairs = [(scale_hbm, scale_ref), (shift_hbm, shift_ref), (we_hbm, we_ref)]
    pairs += [(x_hbm.at[r, pl.ds(0, SPAN)], x_ref.at[r]) for r in range(6)]
    pairs += [(dw_hbm, dw_ref), (wp_hbm, wp_ref)]
    copies = [pltpu.make_async_copy(a, b, sem.at[n]) for n, (a, b) in enumerate(pairs)]
    for copy in copies:
        copy.start()
    clear_edges(e_ref)
    for copy in copies[:3]:
        copy.wait()
    scale, shift = scale_ref[...], shift_ref[...]
    for row in range(6):
        copies[3 + row].wait()
        expand_row(x_ref[row], scale, shift, we_ref, e_ref, row, None)
    for copy in copies[9:]:
        copy.wait()
    taps = dw_ref[...] * 0.5

    def depth(step, carry):
        for row in (2 * step + 1, 2 * step + 2):
            sources = [(e_ref, row - 1), (e_ref, row), (e_ref, row + 1)]
            depth_row(0, sources, x_ref[row, 0:256], taps, wp_ref, mid_ref, row - 1)
        return carry

    lax.fori_loop(0, 2, depth, 0)


def pick_pieces(own_ref, up_ref, down_ref):
    v = own_y()

    def pick(m, carry):
        n_up = v + 1
        row = jnp.minimum(2 * v + m // n_up, 5)
        up_ref[m] = own_ref[row * 4 + jnp.clip(3 - v + lax.rem(m, n_up), 0, 3)]
        n_down = 4 - v
        row = jnp.minimum(m // n_down, 5)
        down_ref[m] = own_ref[row * 4 + lax.rem(m, n_down)]
        return carry

    lax.fori_loop(0, 8, pick, 0)


def expand_halo(half, top_ref, bot_ref, scale, shift, we_ref, e_ref, rows):
    device = lax.axis_index("rows") * 8 + lax.axis_index("cols")
    cols = slice(FIRST[half], FIRST[half] + SPAN)
    for ref, row, present in ((top_ref, rows[0], device > 0), (bot_ref, rows[1], device < 127)):
        expand_row(ref[0, cols], scale, shift, we_ref, e_ref, row, present.astype(F32))


def edge_kernel(
    x_ref, top_ref, bot_ref, e_ref, mid_ref, scale_ref, shift_ref, we_ref, dw_ref, wp_ref,
    own_ref, up_ref, down_ref, halo_ref,
):
    clear_edges(halo_ref)
    expand_halo(0, top_ref, bot_ref, scale_ref[...], shift_ref[...], we_ref, halo_ref, (0, 1))
    taps = dw_ref[...] * 0.5
    sources = [(halo_ref, 0), (e_ref, 0), (e_ref, 1)]
    depth_row(0, sources, x_ref[0, 0:256], taps, wp_ref, own_ref, 0)
    sources = [(e_ref, 4), (e_ref, 5), (halo_ref, 1)]
    depth_row(0, sources, x_ref[5, 0:256], taps, wp_ref, own_ref, 5)

    def keep(m, carry):
        own_ref[4 + m] = mid_ref[m]
        return carry

    lax.fori_loop(0, 16, keep, 0)
    pick_pieces(own_ref, up_ref, down_ref)


def right_kernel(
    x_ref, top_ref, bot_ref, scale_ref, shift_ref, we_ref, dw_ref, wp_ref,
    own_ref, up_ref, down_ref, e_ref,
):
    clear_edges(e_ref)
    scale, shift = scale_ref[...], shift_ref[...]
    expand_halo(1, top_ref, bot_ref, scale, shift, we_ref, e_ref, (0, 7))
    cols = slice(FIRST[1], FIRST[1] + SPAN)

    def expand(step, carry):
        for row in (3 * step, 3 * step + 1, 3 * step + 2):
            expand_row(x_ref[row, cols], scale, shift, we_ref, e_ref, row + 1, None)
        return carry

    lax.fori_loop(0, 2, expand, 0)
    taps = dw_ref[...] * 0.5

    def depth(step, carry):
        for row in (2 * step, 2 * step + 1):
            sources = [(e_ref, row), (e_ref, row + 1), (e_ref, row + 2)]
            depth_row(1, sources, x_ref[row, 256:512], taps, wp_ref, own_ref, row)
        return carry

    lax.fori_loop(0, 3, depth, 0)
    pick_pieces(own_ref, up_ref, down_ref)


def vmem(limit):
    return pltpu.CompilerParams(vmem_limit_bytes=limit * 1024 * 1024)


def pieces(count):
    return jax.ShapeDtypeStruct((count, 4, 16, 256), BF16)


def bottleneck_middle(strips, scale, shift, we, dw, wp):
    return pl.pallas_call(
        middle_kernel,
        out_shape=[pieces(16), jax.ShapeDtypeStruct((6, 8, SPAN + 2 * PAD, 128), F32)],
        in_specs=[pl.BlockSpec(memory_space=pltpu.HBM)] * 6,
        scratch_shapes=[
            pltpu.VMEM((6, SPAN, 256), BF16),
            pltpu.VMEM((1, 256), F32),
            pltpu.VMEM((1, 256), F32),
            pltpu.VMEM((256, 1024), BF16),
            pltpu.VMEM((9, 1024), F32),
            pltpu.VMEM((1024, 256), BF16),
            pltpu.SemaphoreType.DMA((11,)),
        ],
        compiler_params=vmem(24),
        name="bottleneck_middle",
    )(strips, scale, shift, we, dw, wp)


def bottleneck_edge(strips, top, bot, expanded, middle, scale, shift, we, dw, wp):
    return pl.pallas_call(
        edge_kernel,
        out_shape=[pieces(24), pieces(8), pieces(8)],
        scratch_shapes=[pltpu.VMEM((2, 8, SPAN + 2 * PAD, 128), F32)],
        compiler_params=vmem(24),
        name="bottleneck_edge",
    )(strips, top, bot, expanded, middle, scale, shift, we, dw, wp)


def bottleneck_right(strips, top, bot, scale, shift, we, dw, wp):
    return pl.pallas_call(
        right_kernel,
        out_shape=[pieces(24), pieces(8), pieces(8)],
        scratch_shapes=[pltpu.VMEM((8, 8, SPAN + 2 * PAD, 128), F32)],
        compiler_params=vmem(24),
        name="bottleneck_right",
    )(strips, top, bot, scale, shift, we, dw, wp)


def normed_of(x, gain):
    ones = jnp.full((256, 256), 1.0 / 256.0, BF16)
    center = x - jnp.dot(x.astype(BF16), ones, preferred_element_type=F32)
    squares = (center * center).astype(BF16)
    spread = jnp.dot(squares, ones, preferred_element_type=F32)
    return (center * lax.rsqrt(spread + EPSILON) * gain).astype(BF16)


def head_masks(dtype):
    lane = lax.broadcasted_iota(jnp.int32, (1, 128), 1)
    return [(lane // 32 == h).astype(F32).astype(dtype) for h in range(4)]


def attend_and_mix(x, w):
    tokens = x.shape[0]
    masks = head_masks(BF16)
    key_head = lax.broadcasted_iota(jnp.int32, (256, 128), 0) // 64
    lane_head = lax.broadcasted_iota(jnp.int32, (256, 128), 1) // 32
    head_ones = (key_head == lane_head).astype(F32).astype(BF16)
    score_lane = lax.broadcasted_iota(jnp.int32, (64, 256), 1)
    bias = [
        jnp.concatenate([w["bias"][4 * g + h] for h in range(4)], axis=1) * LOG2E
        for g in range(2)
    ]
    normed = normed_of(x, w["gain_a"][...])
    q, k, v = [
        jnp.dot(normed, w["inputs"][:, c * 256 : (c + 1) * 256], preferred_element_type=F32).astype(
            BF16
        )
        for c in range(3)
    ]
    rows = []
    for win in range(tokens // 64):
        at = slice(win * 64, (win + 1) * 64)
        groups = []
        for g in range(2):
            lanes = slice(g * 128, (g + 1) * 128)
            qg, kg, vg = q[at, lanes], k[at, lanes], v[at, lanes]
            keys = jnp.concatenate([kg * masks[h] for h in range(4)], axis=0)
            values = jnp.concatenate([vg * masks[h] for h in range(4)], axis=0)
            values = jnp.concatenate([values, head_ones], axis=1)
            scores = lax.dot_general(
                qg, keys, (((1,), (1,)), ((), ())), preferred_element_type=F32
            )
            scores = scores * (LOG2E * 32**-0.5) + bias[g]
            top = None
            for h in range(4):
                peak = jnp.max(scores[:, h * 64 : (h + 1) * 64], axis=1, keepdims=True)
                top = (
                    jnp.broadcast_to(peak, (64, 256))
                    if top is None
                    else jnp.where(score_lane >= h * 64, peak, top)
                )
            weights = jnp.exp2(scores - top).astype(BF16)
            mixed = jnp.dot(weights, values, preferred_element_type=F32)
            groups.append((mixed[:, :128] * (1.0 / mixed[:, 128:])).astype(BF16))
        rows.append(jnp.concatenate(groups, axis=1))
    combined = jnp.concatenate(rows, axis=0)
    x = x + jnp.dot(combined, w["output"][...], preferred_element_type=F32)
    x = x.astype(BF16).astype(F32)
    normed = normed_of(x, w["gain_m"][...])
    total = jnp.zeros((tokens, 256), F32)
    for c in range(4):
        cols = slice(c * 256, (c + 1) * 256)
        hidden = jnp.dot(normed, w["up"][:, cols], preferred_element_type=F32)
        hidden = twice_gelu(hidden).astype(BF16)
        total = total + jnp.dot(hidden, w["down"][cols, :], preferred_element_type=F32)
    return x + 0.5 * total


NAMES = ("gain_a", "inputs", "output", "bias", "gain_m", "up", "down")


def block_places():
    y = own_y()
    places = []
    for k in range(3):
        n = 3 * y + k
        p = n // 4
        tp = lax.rem(n, 4)
        for s in range(8):
            row = 8 * p + s
            owner = row // 6
            local = row - 6 * owner
            v = jnp.maximum(y - 1, 0)
            m_up = jnp.clip((local - 2 * v) * (v + 1) + tp - (3 - v), 0, 7)
            v = jnp.minimum(y + 1, 3)
            m_down = jnp.clip(local * (4 - v) + tp, 0, 7)
            places.append((owner, local * 4 + tp, m_up, m_down))
    return y, places


def block_kernel(half, own_ref, up_ref, down_ref, *refs):
    w = dict(zip(NAMES, refs))
    refs = refs[len(NAMES) :]
    if half == 1:
        done_ref, out_ref = refs
        out_ref[:, :, 0:4] = done_ref[...]
    else:
        (out_ref,) = refs
    y, places = block_places()
    units = []
    for owner, at, m_up, m_down in places:
        mine = own_ref[at].astype(F32)
        above = up_ref[m_up].astype(F32)
        below = down_ref[m_down].astype(F32)
        units.append(jnp.where(owner == y, mine, jnp.where(owner < y, above, below)))
    windows = [(k, jj, t) for k in range(3) for jj in range(4) for t in range(2)]
    x = jnp.concatenate(
        [units[k * 8 + s][jj, t * 8 : (t + 1) * 8, :] for k, jj, t in windows for s in range(8)],
        axis=0,
    )
    out = attend_and_mix(x, w)
    for k in range(3):
        for jj in range(4):
            first = (k * 4 + jj) * 128
            for s in range(8):
                both = [out[first + t * 64 + s * 8 :][:8] for t in range(2)]
                out_ref[s, k, jj + 4 * half] = jnp.concatenate(both, axis=0).astype(BF16)


def grid_kernel(x_ref, *refs):
    w = dict(zip(NAMES, refs))
    out_ref, flat_ref = refs[len(NAMES) :]

    def slot(k, carry):
        for i in range(8):
            values = x_ref[i, k].astype(F32).reshape(128, 256)
            for half in range(2):
                flat_ref[half, i * 128 : (i + 1) * 128, :] = values[
                    :, half * 128 : (half + 1) * 128
                ]
        windows = []
        for b in range(16):
            at = pl.ds(b, 64, stride=16)
            windows.append(
                jnp.concatenate([flat_ref[half, at, :] for half in range(2)], axis=1)
            )
        out = attend_and_mix(jnp.concatenate(windows, axis=0), w)
        for b in range(16):
            at = pl.ds(b, 64, stride=16)
            for half in range(2):
                flat_ref[half, at, :] = out[
                    b * 64 : (b + 1) * 64, half * 128 : (half + 1) * 128
                ]
        for i in range(8):
            values = jnp.concatenate(
                [flat_ref[half, i * 128 : (i + 1) * 128, :] for half in range(2)], axis=1
            )
            out_ref[pl.ds(i * 8, 8), k] = values.astype(BF16).reshape(8, 16, 256)
        return carry

    lax.fori_loop(0, 3, slot, 0)


def block_section(half, own, up, down, weights, *done):
    return pl.pallas_call(
        functools.partial(block_kernel, half),
        out_shape=jax.ShapeDtypeStruct((8, 3, 4 if half == 0 else 8, 16, 256), BF16),
        compiler_params=vmem(24),
        name="block_section",
    )(own, up, down, *weights, *done)


def grid_section(x, weights):
    return pl.pallas_call(
        grid_kernel,
        out_shape=jax.ShapeDtypeStruct((64, 3, 16, 256), BF16),
        scratch_shapes=[pltpu.VMEM((2, 1024, 128), F32)],
        compiler_params=vmem(24),
        name="grid_section",
    )(x, *weights)


def body(
    stem_strips, norm_scale, norm_shift, expand_weight, depth_weight, project_weight,
    block_gain, block_inputs, block_output, block_bias, first_gain, first_up, first_down,
    grid_gain, grid_inputs, grid_output, grid_bias, second_gain, second_up, second_down,
):
    row = lambda a: a.reshape(1, -1)
    both = ("rows", "cols")
    top = lax.ppermute(stem_strips[5:6], both, STRIP_DOWN)
    bot = lax.ppermute(stem_strips[0:1], both, STRIP_UP)
    weights = (row(norm_scale), row(norm_shift), expand_weight, depth_weight, project_weight)
    middle, expanded = bottleneck_middle(
        *[pltpu.with_memory_space_constraint(a, pltpu.HBM) for a in (stem_strips, *weights)]
    )
    own_l, up_l, down_l = bottleneck_edge(stem_strips, top, bot, expanded, middle, *weights)
    own_l, up_l, down_l, top, bot = lax.optimization_barrier((own_l, up_l, down_l, top, bot))
    up_l, down_l = lax.ppermute(up_l, "cols", Y_UP), lax.ppermute(down_l, "cols", Y_DOWN)
    own_r, up_r, down_r = bottleneck_right(stem_strips, top, bot, *weights)
    up_r, down_r = lax.ppermute(up_r, "cols", Y_UP), lax.ppermute(down_r, "cols", Y_DOWN)
    block_weights = (
        row(block_gain), block_inputs, block_output, block_bias,
        row(first_gain), first_up, first_down,
    )
    grid_weights = (
        row(grid_gain), grid_inputs, grid_output, grid_bias,
        row(second_gain), second_up, second_down,
    )
    left = block_section(0, own_l, up_l, down_l, block_weights)
    sent = block_section(1, own_r, up_r, down_r, block_weights, left)
    arrived = lax.all_to_all(sent, "rows", 0, 0, axis_index_groups=CORE_ROWS, tiled=True)
    back = grid_section(arrived, grid_weights)
    landed = lax.all_to_all(back, both, 0, 0, axis_index_groups=CORE_ALL, tiled=True)
    landed = landed.reshape(8, 2, 3, 4, 16, 256).transpose(1, 2, 0, 3, 4, 5)
    return landed.reshape(48, 64, 256)


def solution(mesh):
    return jax.shard_map(
        body,
        mesh=mesh,
        in_specs=(P(("rows", "cols"), None, None),) + (P(),) * 19,
        out_specs=P("rows", "cols", None),
        check_vma=False,
    )
```

```python
import functools

import jax
import jax.numpy as jnp
from jax import lax
from jax.experimental import pallas as pl
from jax.experimental.pallas import tpu as pltpu
from jax.sharding import PartitionSpec as P

EPSILON = 1e-05
LOG2E = 1.4426950408889634
GELU_A = 0.7978845608028654
GELU_B = GELU_A * 0.044715
F32 = jnp.float32
BF16 = jnp.bfloat16

CORE_ROWS = [[core + 2 * i for i in range(8)] for core in range(2)]
CORE_ALL = [[(core + 2 * i) * 8 + c for i in range(8) for c in range(8)] for core in range(2)]
Y_OUTER = [(c, c ^ 1) for c in range(8)]
Y_INNER = [(c, c // 4 * 4 + (0, 2, 1, 3)[c % 4]) for c in range(8)]
STRIP_NEAR = [(d, d ^ 1) for d in range(128)]
STRIP_FAR = [(d, ((d + 1) ^ 1) - 1 if 0 < d < 127 else 127 - d) for d in range(128)]


def twice_gelu(x):
    inner = x * (GELU_B * (x * x) + GELU_A)
    return x * (1.0 + jnp.tanh(inner))


def own_y():
    return lax.rem(lax.axis_index("cols"), 4)


PAD = 8
SPAN = 272
FIRST = (0, 240)


def twice_gelu_short(x):
    x = x.astype(BF16)
    inner = x * (BF16(GELU_B) * (x * x) + BF16(GELU_A))
    return x * (BF16(1.0) + jnp.tanh(inner))


def clear_edges(e_ref):
    edge = jnp.zeros((PAD, 128), F32)

    def clear(index, carry):
        for lb in range(8):
            e_ref[index, lb, 0:PAD, :] = edge
            e_ref[index, lb, SPAN + PAD : SPAN + 2 * PAD, :] = edge
        return carry

    lax.fori_loop(0, e_ref.shape[0], clear, 0)


def expand_row(values, scale, shift, we_ref, e_ref, row, factor):
    normed = (values.astype(F32) * scale + shift).astype(BF16)
    for nb in range(4):
        flat = jnp.dot(normed, we_ref[:, nb * 256 : (nb + 1) * 256], preferred_element_type=F32)
        wide = twice_gelu(flat)
        if factor is not None:
            wide = wide * factor
        for part in range(2):
            e_ref[row, nb * 2 + part, PAD : SPAN + PAD, :] = wide[:, part * 128 : (part + 1) * 128]


def depth_row(half, sources, values, taps, wp_ref, out_ref, at_row):
    base = 256 * half - FIRST[half] + PAD
    total = jnp.zeros((256, 256), F32)
    for pair in range(4):
        parts = []
        for lb in (2 * pair, 2 * pair + 1):
            acc = None
            for tap in range(9):
                e_ref, at = sources[tap // 3]
                term = (
                    e_ref[at, lb, pl.ds(base - 1 + tap % 3, 256), :]
                    * taps[tap : tap + 1, lb * 128 : (lb + 1) * 128]
                )
                acc = term if acc is None else acc + term
            parts.append(twice_gelu_short(acc))
        wide = jnp.concatenate(parts, axis=1)
        total = total + jnp.dot(
            wide, wp_ref[pair * 256 : (pair + 1) * 256, :], preferred_element_type=F32
        )
    result = (values.astype(F32) + 0.5 * total).astype(BF16)
    for jj in range(4):
        for tp in range(4):
            at = jj * 64 + tp * 16
            out_ref[at_row * 4 + tp, jj] = result[at : at + 16]


def middle_kernel(
    x_hbm, scale_hbm, shift_hbm, we_hbm, dw_hbm, wp_hbm, mid_ref, e_ref,
    x_ref, scale_ref, shift_ref, we_ref, dw_ref, wp_ref, sem,
):
    pairs = [(scale_hbm, scale_ref), (shift_hbm, shift_ref), (we_hbm, we_ref)]
    pairs += [(x_hbm.at[r, pl.ds(0, SPAN)], x_ref.at[r]) for r in range(6)]
    pairs += [(dw_hbm, dw_ref), (wp_hbm, wp_ref)]
    copies = [pltpu.make_async_copy(a, b, sem.at[n]) for n, (a, b) in enumerate(pairs)]
    for copy in copies:
        copy.start()
    clear_edges(e_ref)
    for copy in copies[:3]:
        copy.wait()
    scale, shift = scale_ref[...], shift_ref[...]
    for row in range(6):
        copies[3 + row].wait()
        expand_row(x_ref[row], scale, shift, we_ref, e_ref, row, None)
    for copy in copies[9:]:
        copy.wait()
    taps = dw_ref[...] * 0.5

    def depth(step, carry):
        for row in (2 * step + 1, 2 * step + 2):
            sources = [(e_ref, row - 1), (e_ref, row), (e_ref, row + 1)]
            depth_row(0, sources, x_ref[row, 0:256], taps, wp_ref, mid_ref, row - 1)
        return carry

    lax.fori_loop(0, 2, depth, 0)


def pick_pieces(own_ref, outer_ref, inner_ref):
    v = own_y()

    def pick(m, up):
        wide = jnp.where(up, v + 1, 4 - v)
        first = jnp.where(up, 2 * v, 0)
        row = jnp.minimum(first + m // wide, 5)
        tp = jnp.clip(jnp.where(up, 3 - v, 0) + lax.rem(m, wide), 0, 3)
        return own_ref[row * 4 + tp]

    def pick_outer(m, carry):
        outer_ref[m] = pick(m, lax.rem(v, 2) == 0)
        return carry

    def pick_inner(m, carry):
        inner_ref[m] = pick(m, v < 2)
        return carry

    lax.fori_loop(0, 6, pick_outer, 0)
    lax.fori_loop(0, 8, pick_inner, 0)


def expand_halo(half, near_ref, far_ref, scale, shift, we_ref, e_ref, rows):
    device = lax.axis_index("rows") * 8 + lax.axis_index("cols")
    even = lax.rem(device, 2) == 0
    cols = slice(FIRST[half], FIRST[half] + SPAN)
    above, below = rows
    row = jnp.where(even, below, above)
    expand_row(near_ref[0, cols], scale, shift, we_ref, e_ref, row, None)
    inside = jnp.logical_and(device > 0, device < 127).astype(F32)
    row = jnp.where(even, above, below)
    expand_row(far_ref[0, cols], scale, shift, we_ref, e_ref, row, inside)


def edge_kernel(
    x_ref, near_ref, far_ref, e_ref, mid_ref, scale_ref, shift_ref, we_ref, dw_ref, wp_ref,
    own_ref, outer_ref, inner_ref, halo_ref,
):
    clear_edges(halo_ref)
    expand_halo(0, near_ref, far_ref, scale_ref[...], shift_ref[...], we_ref, halo_ref, (0, 1))
    taps = dw_ref[...] * 0.5
    sources = [(halo_ref, 0), (e_ref, 0), (e_ref, 1)]
    depth_row(0, sources, x_ref[0, 0:256], taps, wp_ref, own_ref, 0)
    sources = [(e_ref, 4), (e_ref, 5), (halo_ref, 1)]
    depth_row(0, sources, x_ref[5, 0:256], taps, wp_ref, own_ref, 5)

    def keep(m, carry):
        own_ref[4 + m] = mid_ref[m]
        return carry

    lax.fori_loop(0, 16, keep, 0)
    pick_pieces(own_ref, outer_ref, inner_ref)


def right_kernel(
    x_ref, near_ref, far_ref, scale_ref, shift_ref, we_ref, dw_ref, wp_ref,
    own_ref, outer_ref, inner_ref, e_ref,
):
    clear_edges(e_ref)
    scale, shift = scale_ref[...], shift_ref[...]
    expand_halo(1, near_ref, far_ref, scale, shift, we_ref, e_ref, (0, 7))
    cols = slice(FIRST[1], FIRST[1] + SPAN)

    def expand(step, carry):
        for row in (3 * step, 3 * step + 1, 3 * step + 2):
            expand_row(x_ref[row, cols], scale, shift, we_ref, e_ref, row + 1, None)
        return carry

    lax.fori_loop(0, 2, expand, 0)
    taps = dw_ref[...] * 0.5

    def depth(step, carry):
        for row in (2 * step, 2 * step + 1):
            sources = [(e_ref, row), (e_ref, row + 1), (e_ref, row + 2)]
            depth_row(1, sources, x_ref[row, 256:512], taps, wp_ref, own_ref, row)
        return carry

    lax.fori_loop(0, 3, depth, 0)
    pick_pieces(own_ref, outer_ref, inner_ref)


def vmem(limit):
    return pltpu.CompilerParams(vmem_limit_bytes=limit * 1024 * 1024)


def pieces(count):
    return jax.ShapeDtypeStruct((count, 4, 16, 256), BF16)


def bottleneck_middle(strips, scale, shift, we, dw, wp):
    return pl.pallas_call(
        middle_kernel,
        out_shape=[pieces(16), jax.ShapeDtypeStruct((6, 8, SPAN + 2 * PAD, 128), F32)],
        in_specs=[pl.BlockSpec(memory_space=pltpu.HBM)] * 6,
        scratch_shapes=[
            pltpu.VMEM((6, SPAN, 256), BF16),
            pltpu.VMEM((1, 256), F32),
            pltpu.VMEM((1, 256), F32),
            pltpu.VMEM((256, 1024), BF16),
            pltpu.VMEM((9, 1024), F32),
            pltpu.VMEM((1024, 256), BF16),
            pltpu.SemaphoreType.DMA((11,)),
        ],
        compiler_params=vmem(24),
        name="bottleneck_middle",
    )(strips, scale, shift, we, dw, wp)


def bottleneck_edge(strips, near, far, expanded, middle, scale, shift, we, dw, wp):
    return pl.pallas_call(
        edge_kernel,
        out_shape=[pieces(24), pieces(6), pieces(8)],
        scratch_shapes=[pltpu.VMEM((2, 8, SPAN + 2 * PAD, 128), F32)],
        compiler_params=vmem(24),
        name="bottleneck_edge",
    )(strips, near, far, expanded, middle, scale, shift, we, dw, wp)


def bottleneck_right(strips, near, far, scale, shift, we, dw, wp):
    return pl.pallas_call(
        right_kernel,
        out_shape=[pieces(24), pieces(6), pieces(8)],
        scratch_shapes=[pltpu.VMEM((8, 8, SPAN + 2 * PAD, 128), F32)],
        compiler_params=vmem(24),
        name="bottleneck_right",
    )(strips, near, far, scale, shift, we, dw, wp)


def normed_of(x, gain):
    ones = jnp.full((256, 256), 1.0 / 256.0, BF16)
    center = x - jnp.dot(x.astype(BF16), ones, preferred_element_type=F32)
    squares = (center * center).astype(BF16)
    spread = jnp.dot(squares, ones, preferred_element_type=F32)
    return (center * lax.rsqrt(spread + EPSILON) * gain).astype(BF16)


def head_masks(dtype):
    lane = lax.broadcasted_iota(jnp.int32, (1, 128), 1)
    return [(lane // 32 == h).astype(F32).astype(dtype) for h in range(4)]


def attend_and_mix(x, w):
    tokens = x.shape[0]
    masks = head_masks(BF16)
    key_head = lax.broadcasted_iota(jnp.int32, (256, 128), 0) // 64
    lane_head = lax.broadcasted_iota(jnp.int32, (256, 128), 1) // 32
    head_ones = (key_head == lane_head).astype(F32).astype(BF16)
    score_lane = lax.broadcasted_iota(jnp.int32, (64, 256), 1)
    bias = [
        jnp.concatenate([w["bias"][4 * g + h] for h in range(4)], axis=1) * LOG2E
        for g in range(2)
    ]
    normed = normed_of(x, w["gain_a"][...])
    q, k, v = [
        jnp.dot(normed, w["inputs"][:, c * 256 : (c + 1) * 256], preferred_element_type=F32).astype(
            BF16
        )
        for c in range(3)
    ]
    rows = []
    for win in range(tokens // 64):
        at = slice(win * 64, (win + 1) * 64)
        groups = []
        for g in range(2):
            lanes = slice(g * 128, (g + 1) * 128)
            qg, kg, vg = q[at, lanes], k[at, lanes], v[at, lanes]
            keys = jnp.concatenate([kg * masks[h] for h in range(4)], axis=0)
            values = jnp.concatenate([vg * masks[h] for h in range(4)], axis=0)
            values = jnp.concatenate([values, head_ones], axis=1)
            scores = lax.dot_general(
                qg, keys, (((1,), (1,)), ((), ())), preferred_element_type=F32
            )
            scores = scores * (LOG2E * 32**-0.5) + bias[g]
            top = None
            for h in range(4):
                peak = jnp.max(scores[:, h * 64 : (h + 1) * 64], axis=1, keepdims=True)
                top = (
                    jnp.broadcast_to(peak, (64, 256))
                    if top is None
                    else jnp.where(score_lane >= h * 64, peak, top)
                )
            weights = jnp.exp2(scores - top).astype(BF16)
            mixed = jnp.dot(weights, values, preferred_element_type=F32)
            groups.append((mixed[:, :128] * (1.0 / mixed[:, 128:])).astype(BF16))
        rows.append(jnp.concatenate(groups, axis=1))
    combined = jnp.concatenate(rows, axis=0)
    x = x + jnp.dot(combined, w["output"][...], preferred_element_type=F32)
    x = x.astype(BF16).astype(F32)
    normed = normed_of(x, w["gain_m"][...])
    total = jnp.zeros((tokens, 256), F32)
    for c in range(4):
        cols = slice(c * 256, (c + 1) * 256)
        hidden = jnp.dot(normed, w["up"][:, cols], preferred_element_type=F32)
        hidden = twice_gelu(hidden).astype(BF16)
        total = total + jnp.dot(hidden, w["down"][cols, :], preferred_element_type=F32)
    return x + 0.5 * total


NAMES = ("gain_a", "inputs", "output", "bias", "gain_m", "up", "down")


def block_places():
    y = own_y()
    places = []
    for k in range(3):
        n = 3 * y + k
        p = n // 4
        tp = lax.rem(n, 4)
        for s in range(8):
            row = 8 * p + s
            owner = row // 6
            local = row - 6 * owner
            v = jnp.maximum(y - 1, 0)
            m_up = (local - 2 * v) * (v + 1) + tp - (3 - v)
            v = jnp.minimum(y + 1, 3)
            m = jnp.where(owner < y, m_up, local * (4 - v) + tp)
            outer = owner // 2 == y // 2
            places.append((owner, local * 4 + tp, outer, jnp.clip(m, 0, 5), jnp.clip(m, 0, 7)))
    return y, places


def block_kernel(half, own_ref, outer_ref, inner_ref, *refs):
    w = dict(zip(NAMES, refs))
    refs = refs[len(NAMES) :]
    if half == 1:
        done_ref, out_ref = refs
        out_ref[:, :, 0:4] = done_ref[...]
    else:
        (out_ref,) = refs
    y, places = block_places()
    units = []
    for owner, at, outer, m_outer, m_inner in places:
        mine = own_ref[at].astype(F32)
        one = outer_ref[m_outer].astype(F32)
        two = inner_ref[m_inner].astype(F32)
        units.append(jnp.where(owner == y, mine, jnp.where(outer, one, two)))
    windows = [(k, jj, t) for k in range(3) for jj in range(4) for t in range(2)]
    x = jnp.concatenate(
        [units[k * 8 + s][jj, t * 8 : (t + 1) * 8, :] for k, jj, t in windows for s in range(8)],
        axis=0,
    )
    out = attend_and_mix(x, w)
    for k in range(3):
        for jj in range(4):
            first = (k * 4 + jj) * 128
            for s in range(8):
                both = [out[first + t * 64 + s * 8 :][:8] for t in range(2)]
                out_ref[s, k, jj + 4 * half] = jnp.concatenate(both, axis=0).astype(BF16)


def grid_kernel(x_ref, *refs):
    w = dict(zip(NAMES, refs))
    out_ref, flat_ref = refs[len(NAMES) :]

    def slot(k, carry):
        for i in range(8):
            values = x_ref[i, k].astype(F32).reshape(128, 256)
            for half in range(2):
                flat_ref[half, i * 128 : (i + 1) * 128, :] = values[
                    :, half * 128 : (half + 1) * 128
                ]
        windows = []
        for b in range(16):
            at = pl.ds(b, 64, stride=16)
            windows.append(
                jnp.concatenate([flat_ref[half, at, :] for half in range(2)], axis=1)
            )
        out = attend_and_mix(jnp.concatenate(windows, axis=0), w)
        for b in range(16):
            at = pl.ds(b, 64, stride=16)
            for half in range(2):
                flat_ref[half, at, :] = out[
                    b * 64 : (b + 1) * 64, half * 128 : (half + 1) * 128
                ]
        for i in range(8):
            values = jnp.concatenate(
                [flat_ref[half, i * 128 : (i + 1) * 128, :] for half in range(2)], axis=1
            )
            out_ref[pl.ds(i * 8, 8), k] = values.astype(BF16).reshape(8, 16, 256)
        return carry

    lax.fori_loop(0, 3, slot, 0)


def block_section(half, own, outer, inner, weights, *done):
    return pl.pallas_call(
        functools.partial(block_kernel, half),
        out_shape=jax.ShapeDtypeStruct((8, 3, 4 if half == 0 else 8, 16, 256), BF16),
        compiler_params=vmem(24),
        name="block_section",
    )(own, outer, inner, *weights, *done)


def grid_section(x, weights):
    return pl.pallas_call(
        grid_kernel,
        out_shape=jax.ShapeDtypeStruct((64, 3, 16, 256), BF16),
        scratch_shapes=[pltpu.VMEM((2, 1024, 128), F32)],
        compiler_params=vmem(24),
        name="grid_section",
    )(x, *weights)


def body(
    stem_strips, norm_scale, norm_shift, expand_weight, depth_weight, project_weight,
    block_gain, block_inputs, block_output, block_bias, first_gain, first_up, first_down,
    grid_gain, grid_inputs, grid_output, grid_bias, second_gain, second_up, second_down,
):
    row = lambda a: a.reshape(1, -1)
    both = ("rows", "cols")
    even = lax.rem(lax.axis_index("cols"), 2) == 0
    first, last = stem_strips[0:1], stem_strips[5:6]
    near = lax.ppermute(jnp.where(even, last, first), both, STRIP_NEAR)
    far = lax.ppermute(jnp.where(even, first, last), both, STRIP_FAR)
    weights = (row(norm_scale), row(norm_shift), expand_weight, depth_weight, project_weight)
    middle, expanded = bottleneck_middle(
        *[pltpu.with_memory_space_constraint(a, pltpu.HBM) for a in (stem_strips, *weights)]
    )
    own_l, outer_l, inner_l = bottleneck_edge(stem_strips, near, far, expanded, middle, *weights)
    own_l, outer_l, inner_l, near, far = lax.optimization_barrier((own_l, outer_l, inner_l, near, far))
    outer_l = lax.ppermute(outer_l, "cols", Y_OUTER)
    inner_l = lax.ppermute(inner_l, "cols", Y_INNER)
    own_r, outer_r, inner_r = bottleneck_right(stem_strips, near, far, *weights)
    outer_l, inner_l, outer_r, inner_r = lax.optimization_barrier(
        (outer_l, inner_l, outer_r, inner_r)
    )
    outer_r = lax.ppermute(outer_r, "cols", Y_OUTER)
    inner_r = lax.ppermute(inner_r, "cols", Y_INNER)
    block_weights = (
        row(block_gain), block_inputs, block_output, block_bias,
        row(first_gain), first_up, first_down,
    )
    grid_weights = (
        row(grid_gain), grid_inputs, grid_output, grid_bias,
        row(second_gain), second_up, second_down,
    )
    left = block_section(0, own_l, outer_l, inner_l, block_weights)
    sent = block_section(1, own_r, outer_r, inner_r, block_weights, left)
    arrived = lax.all_to_all(sent, "rows", 0, 0, axis_index_groups=CORE_ROWS, tiled=True)
    back = grid_section(arrived, grid_weights)
    landed = lax.all_to_all(back, both, 0, 0, axis_index_groups=CORE_ALL, tiled=True)
    landed = landed.reshape(8, 2, 3, 4, 16, 256).transpose(1, 2, 0, 3, 4, 5)
    return landed.reshape(48, 64, 256)


def solution(mesh):
    return jax.shard_map(
        body,
        mesh=mesh,
        in_specs=(P(("rows", "cols"), None, None),) + (P(),) * 19,
        out_specs=P("rows", "cols", None),
        check_vma=False,
    )
```

```python
import functools

import jax
import jax.numpy as jnp
from jax import lax
from jax.experimental import pallas as pl
from jax.experimental.pallas import tpu as pltpu
from jax.sharding import PartitionSpec as P

EPSILON = 1e-05
LOG2E = 1.4426950408889634
GELU_A = 0.7978845608028654
GELU_B = GELU_A * 0.044715
F32 = jnp.float32
BF16 = jnp.bfloat16

CORE_ROWS = [[core + 2 * i for i in range(8)] for core in range(2)]
CORE_ALL = [[(core + 2 * i) * 8 + c for i in range(8) for c in range(8)] for core in range(2)]
Y_OUTER = [(c, c ^ 1) for c in range(8)]
Y_INNER = [(c, c // 4 * 4 + (0, 2, 1, 3)[c % 4]) for c in range(8)]
STRIP_NEAR = [(d, d ^ 1) for d in range(128)]
STRIP_FAR = [(d, ((d + 1) ^ 1) - 1 if 0 < d < 127 else 127 - d) for d in range(128)]


def twice_gelu(x):
    inner = x * (GELU_B * (x * x) + GELU_A)
    return x * (1.0 + jnp.tanh(inner))


def own_y():
    return lax.rem(lax.axis_index("cols"), 4)


PAD = 8
SPAN = 272
FIRST = (0, 240)


def twice_gelu_short(x):
    x = x.astype(BF16)
    inner = x * (BF16(GELU_B) * (x * x) + BF16(GELU_A))
    return x * (BF16(1.0) + jnp.tanh(inner))


def clear_edges(e_ref):
    edge = jnp.zeros((PAD, 128), F32)

    def clear(index, carry):
        for lb in range(8):
            e_ref[index, lb, 0:PAD, :] = edge
            e_ref[index, lb, SPAN + PAD : SPAN + 2 * PAD, :] = edge
        return carry

    lax.fori_loop(0, e_ref.shape[0], clear, 0)


def expand_row(values, scale, shift, we_ref, e_ref, row, factor):
    normed = (values.astype(F32) * scale + shift).astype(BF16)
    for nb in range(4):
        flat = jnp.dot(normed, we_ref[:, nb * 256 : (nb + 1) * 256], preferred_element_type=F32)
        wide = twice_gelu(flat)
        if factor is not None:
            wide = wide * factor
        for part in range(2):
            e_ref[row, nb * 2 + part, PAD : SPAN + PAD, :] = wide[:, part * 128 : (part + 1) * 128]


def depth_row(half, sources, values, taps, wp_ref, out_ref, at_row):
    base = 256 * half - FIRST[half] + PAD
    total = jnp.zeros((256, 256), F32)
    for pair in range(4):
        parts = []
        for lb in (2 * pair, 2 * pair + 1):
            acc = None
            for tap in range(9):
                e_ref, at = sources[tap // 3]
                term = (
                    e_ref[at, lb, pl.ds(base - 1 + tap % 3, 256), :]
                    * taps[tap : tap + 1, lb * 128 : (lb + 1) * 128]
                )
                acc = term if acc is None else acc + term
            parts.append(twice_gelu_short(acc))
        wide = jnp.concatenate(parts, axis=1)
        total = total + jnp.dot(
            wide, wp_ref[pair * 256 : (pair + 1) * 256, :], preferred_element_type=F32
        )
    result = (values.astype(F32) + 0.5 * total).astype(BF16)
    for jj in range(4):
        for tp in range(4):
            at = jj * 64 + tp * 16
            out_ref[at_row * 4 + tp, jj] = result[at : at + 16]


def middle_kernel(
    x_hbm, scale_hbm, shift_hbm, we_hbm, dw_hbm, wp_hbm, mid_ref, e_ref,
    x_ref, scale_ref, shift_ref, we_ref, dw_ref, wp_ref, sem,
):
    pairs = [(scale_hbm, scale_ref), (shift_hbm, shift_ref), (we_hbm, we_ref)]
    pairs += [(x_hbm.at[r, pl.ds(0, SPAN)], x_ref.at[r]) for r in range(6)]
    pairs += [(dw_hbm, dw_ref), (wp_hbm, wp_ref)]
    copies = [pltpu.make_async_copy(a, b, sem.at[n]) for n, (a, b) in enumerate(pairs)]
    for copy in copies:
        copy.start()
    clear_edges(e_ref)
    for copy in copies[:3]:
        copy.wait()
    scale, shift = scale_ref[...], shift_ref[...]
    for row in range(6):
        copies[3 + row].wait()
        expand_row(x_ref[row], scale, shift, we_ref, e_ref, row, None)
    for copy in copies[9:]:
        copy.wait()
    taps = dw_ref[...] * 0.5

    def depth(step, carry):
        for row in (2 * step + 1, 2 * step + 2):
            sources = [(e_ref, row - 1), (e_ref, row), (e_ref, row + 1)]
            depth_row(0, sources, x_ref[row, 0:256], taps, wp_ref, mid_ref, row - 1)
        return carry

    lax.fori_loop(0, 2, depth, 0)


def pick_pieces(own_ref, outer_ref, inner_ref):
    v = own_y()

    def pick(m, up):
        wide = jnp.where(up, v + 1, 4 - v)
        first = jnp.where(up, 2 * v, 0)
        row = jnp.minimum(first + m // wide, 5)
        tp = jnp.clip(jnp.where(up, 3 - v, 0) + lax.rem(m, wide), 0, 3)
        return own_ref[row * 4 + tp]

    def pick_outer(m, carry):
        outer_ref[m] = pick(m, lax.rem(v, 2) == 0)
        return carry

    def pick_inner(m, carry):
        inner_ref[m] = pick(m, v < 2)
        return carry

    lax.fori_loop(0, 6, pick_outer, 0)
    lax.fori_loop(0, 8, pick_inner, 0)


def expand_halo(half, near_ref, far_ref, scale, shift, we_ref, e_ref, rows):
    device = lax.axis_index("rows") * 8 + lax.axis_index("cols")
    even = lax.rem(device, 2) == 0
    cols = slice(FIRST[half], FIRST[half] + SPAN)
    above, below = rows
    row = jnp.where(even, below, above)
    expand_row(near_ref[0, cols], scale, shift, we_ref, e_ref, row, None)
    inside = jnp.logical_and(device > 0, device < 127).astype(F32)
    row = jnp.where(even, above, below)
    expand_row(far_ref[0, cols], scale, shift, we_ref, e_ref, row, inside)


def edge_kernel(
    x_ref, near_ref, far_ref, e_ref, mid_ref, scale_ref, shift_ref, we_ref, dw_ref, wp_ref,
    own_ref, outer_ref, inner_ref, halo_ref,
):
    clear_edges(halo_ref)
    expand_halo(0, near_ref, far_ref, scale_ref[...], shift_ref[...], we_ref, halo_ref, (0, 1))
    taps = dw_ref[...] * 0.5
    sources = [(halo_ref, 0), (e_ref, 0), (e_ref, 1)]
    depth_row(0, sources, x_ref[0, 0:256], taps, wp_ref, own_ref, 0)
    sources = [(e_ref, 4), (e_ref, 5), (halo_ref, 1)]
    depth_row(0, sources, x_ref[5, 0:256], taps, wp_ref, own_ref, 5)

    def keep(m, carry):
        own_ref[4 + m] = mid_ref[m]
        return carry

    lax.fori_loop(0, 16, keep, 0)
    pick_pieces(own_ref, outer_ref, inner_ref)


def right_kernel(
    x_ref, near_ref, far_ref, scale_ref, shift_ref, we_ref, dw_ref, wp_ref,
    own_ref, outer_ref, inner_ref, e_ref,
):
    clear_edges(e_ref)
    scale, shift = scale_ref[...], shift_ref[...]
    expand_halo(1, near_ref, far_ref, scale, shift, we_ref, e_ref, (0, 7))
    cols = slice(FIRST[1], FIRST[1] + SPAN)

    def expand(step, carry):
        for row in (3 * step, 3 * step + 1, 3 * step + 2):
            expand_row(x_ref[row, cols], scale, shift, we_ref, e_ref, row + 1, None)
        return carry

    lax.fori_loop(0, 2, expand, 0)
    taps = dw_ref[...] * 0.5

    def depth(step, carry):
        for row in (2 * step, 2 * step + 1):
            sources = [(e_ref, row), (e_ref, row + 1), (e_ref, row + 2)]
            depth_row(1, sources, x_ref[row, 256:512], taps, wp_ref, own_ref, row)
        return carry

    lax.fori_loop(0, 3, depth, 0)
    pick_pieces(own_ref, outer_ref, inner_ref)


def vmem(limit):
    return pltpu.CompilerParams(vmem_limit_bytes=limit * 1024 * 1024)


def pieces(count):
    return jax.ShapeDtypeStruct((count, 4, 16, 256), BF16)


def bottleneck_middle(strips, scale, shift, we, dw, wp):
    return pl.pallas_call(
        middle_kernel,
        out_shape=[pieces(16), jax.ShapeDtypeStruct((6, 8, SPAN + 2 * PAD, 128), F32)],
        in_specs=[pl.BlockSpec(memory_space=pltpu.HBM)] * 6,
        scratch_shapes=[
            pltpu.VMEM((6, SPAN, 256), BF16),
            pltpu.VMEM((1, 256), F32),
            pltpu.VMEM((1, 256), F32),
            pltpu.VMEM((256, 1024), BF16),
            pltpu.VMEM((9, 1024), F32),
            pltpu.VMEM((1024, 256), BF16),
            pltpu.SemaphoreType.DMA((11,)),
        ],
        compiler_params=vmem(24),
        name="bottleneck_middle",
    )(strips, scale, shift, we, dw, wp)


def bottleneck_edge(strips, near, far, expanded, middle, scale, shift, we, dw, wp):
    return pl.pallas_call(
        edge_kernel,
        out_shape=[pieces(24), pieces(6), pieces(8)],
        scratch_shapes=[pltpu.VMEM((2, 8, SPAN + 2 * PAD, 128), F32)],
        compiler_params=vmem(24),
        name="bottleneck_edge",
    )(strips, near, far, expanded, middle, scale, shift, we, dw, wp)


def bottleneck_right(strips, near, far, scale, shift, we, dw, wp):
    return pl.pallas_call(
        right_kernel,
        out_shape=[pieces(24), pieces(6), pieces(8)],
        scratch_shapes=[pltpu.VMEM((8, 8, SPAN + 2 * PAD, 128), F32)],
        compiler_params=vmem(24),
        name="bottleneck_right",
    )(strips, near, far, scale, shift, we, dw, wp)


def normed_of(x, gain):
    ones = jnp.full((256, 256), 1.0 / 256.0, BF16)
    center = x - jnp.dot(x.astype(BF16), ones, preferred_element_type=F32)
    squares = (center * center).astype(BF16)
    spread = jnp.dot(squares, ones, preferred_element_type=F32)
    return (center * lax.rsqrt(spread + EPSILON) * gain).astype(BF16)


def head_masks(dtype):
    lane = lax.broadcasted_iota(jnp.int32, (1, 128), 1)
    return [(lane // 32 == h).astype(F32).astype(dtype) for h in range(4)]


def attend_and_mix(x, w):
    tokens = x.shape[0]
    masks = head_masks(BF16)
    key_head = lax.broadcasted_iota(jnp.int32, (256, 128), 0) // 64
    lane_head = lax.broadcasted_iota(jnp.int32, (256, 128), 1) // 32
    head_ones = (key_head == lane_head).astype(F32).astype(BF16)
    score_lane = lax.broadcasted_iota(jnp.int32, (64, 256), 1)
    bias = [
        jnp.concatenate([w["bias"][4 * g + h] for h in range(4)], axis=1) * LOG2E
        for g in range(2)
    ]
    normed = normed_of(x, w["gain_a"][...])
    q, k, v = [
        jnp.dot(normed, w["inputs"][:, c * 256 : (c + 1) * 256], preferred_element_type=F32).astype(
            BF16
        )
        for c in range(3)
    ]
    rows = []
    for win in range(tokens // 64):
        at = slice(win * 64, (win + 1) * 64)
        groups = []
        for g in range(2):
            lanes = slice(g * 128, (g + 1) * 128)
            qg, kg, vg = q[at, lanes], k[at, lanes], v[at, lanes]
            keys = jnp.concatenate([kg * masks[h] for h in range(4)], axis=0)
            values = jnp.concatenate([vg * masks[h] for h in range(4)], axis=0)
            values = jnp.concatenate([values, head_ones], axis=1)
            scores = lax.dot_general(
                qg, keys, (((1,), (1,)), ((), ())), preferred_element_type=F32
            )
            scores = scores * (LOG2E * 32**-0.5) + bias[g]
            top = None
            for h in range(4):
                peak = jnp.max(scores[:, h * 64 : (h + 1) * 64], axis=1, keepdims=True)
                top = (
                    jnp.broadcast_to(peak, (64, 256))
                    if top is None
                    else jnp.where(score_lane >= h * 64, peak, top)
                )
            weights = jnp.exp2(scores - top).astype(BF16)
            mixed = jnp.dot(weights, values, preferred_element_type=F32)
            groups.append((mixed[:, :128] * (1.0 / mixed[:, 128:])).astype(BF16))
        rows.append(jnp.concatenate(groups, axis=1))
    combined = jnp.concatenate(rows, axis=0)
    x = x + jnp.dot(combined, w["output"][...], preferred_element_type=F32)
    x = x.astype(BF16).astype(F32)
    normed = normed_of(x, w["gain_m"][...])
    total = jnp.zeros((tokens, 256), F32)
    for c in range(4):
        cols = slice(c * 256, (c + 1) * 256)
        hidden = jnp.dot(normed, w["up"][:, cols], preferred_element_type=F32)
        hidden = twice_gelu_short(hidden)
        total = total + jnp.dot(hidden, w["down"][cols, :], preferred_element_type=F32)
    return x + 0.5 * total


NAMES = ("gain_a", "inputs", "output", "bias", "gain_m", "up", "down")


def block_places():
    y = own_y()
    places = []
    for k in range(3):
        n = 3 * y + k
        p = n // 4
        tp = lax.rem(n, 4)
        for s in range(8):
            row = 8 * p + s
            owner = row // 6
            local = row - 6 * owner
            v = jnp.maximum(y - 1, 0)
            m_up = (local - 2 * v) * (v + 1) + tp - (3 - v)
            v = jnp.minimum(y + 1, 3)
            m = jnp.where(owner < y, m_up, local * (4 - v) + tp)
            outer = owner // 2 == y // 2
            places.append((owner, local * 4 + tp, outer, jnp.clip(m, 0, 5), jnp.clip(m, 0, 7)))
    return y, places


def block_kernel(half, own_ref, outer_ref, inner_ref, *refs):
    w = dict(zip(NAMES, refs))
    refs = refs[len(NAMES) :]
    if half == 1:
        done_ref, out_ref = refs
        out_ref[:, :, 0:4] = done_ref[...]
    else:
        (out_ref,) = refs
    y, places = block_places()
    units = []
    for owner, at, outer, m_outer, m_inner in places:
        mine = own_ref[at].astype(F32)
        one = outer_ref[m_outer].astype(F32)
        two = inner_ref[m_inner].astype(F32)
        units.append(jnp.where(owner == y, mine, jnp.where(outer, one, two)))
    windows = [(k, jj, t) for k in range(3) for jj in range(4) for t in range(2)]
    x = jnp.concatenate(
        [units[k * 8 + s][jj, t * 8 : (t + 1) * 8, :] for k, jj, t in windows for s in range(8)],
        axis=0,
    )
    out = attend_and_mix(x, w)
    for k in range(3):
        for jj in range(4):
            first = (k * 4 + jj) * 128
            for s in range(8):
                both = [out[first + t * 64 + s * 8 :][:8] for t in range(2)]
                out_ref[s, k, jj + 4 * half] = jnp.concatenate(both, axis=0).astype(BF16)


def grid_kernel(x_ref, *refs):
    w = dict(zip(NAMES, refs))
    out_ref, flat_ref = refs[len(NAMES) :]

    def slot(k, carry):
        for i in range(8):
            values = x_ref[i, k].astype(F32).reshape(128, 256)
            for half in range(2):
                flat_ref[half, i * 128 : (i + 1) * 128, :] = values[
                    :, half * 128 : (half + 1) * 128
                ]
        windows = []
        for b in range(16):
            at = pl.ds(b, 64, stride=16)
            windows.append(
                jnp.concatenate([flat_ref[half, at, :] for half in range(2)], axis=1)
            )
        out = attend_and_mix(jnp.concatenate(windows, axis=0), w)
        for b in range(16):
            at = pl.ds(b, 64, stride=16)
            for half in range(2):
                flat_ref[half, at, :] = out[
                    b * 64 : (b + 1) * 64, half * 128 : (half + 1) * 128
                ]
        for i in range(8):
            values = jnp.concatenate(
                [flat_ref[half, i * 128 : (i + 1) * 128, :] for half in range(2)], axis=1
            )
            out_ref[pl.ds(i * 8, 8), k] = values.astype(BF16).reshape(8, 16, 256)
        return carry

    lax.fori_loop(0, 3, slot, 0)


def block_section(half, own, outer, inner, weights, *done):
    return pl.pallas_call(
        functools.partial(block_kernel, half),
        out_shape=jax.ShapeDtypeStruct((8, 3, 4 if half == 0 else 8, 16, 256), BF16),
        compiler_params=vmem(24),
        name="block_section",
    )(own, outer, inner, *weights, *done)


def grid_section(x, weights):
    return pl.pallas_call(
        grid_kernel,
        out_shape=jax.ShapeDtypeStruct((64, 3, 16, 256), BF16),
        scratch_shapes=[pltpu.VMEM((2, 1024, 128), F32)],
        compiler_params=vmem(24),
        name="grid_section",
    )(x, *weights)


def body(
    stem_strips, norm_scale, norm_shift, expand_weight, depth_weight, project_weight,
    block_gain, block_inputs, block_output, block_bias, first_gain, first_up, first_down,
    grid_gain, grid_inputs, grid_output, grid_bias, second_gain, second_up, second_down,
):
    row = lambda a: a.reshape(1, -1)
    both = ("rows", "cols")
    even = lax.rem(lax.axis_index("cols"), 2) == 0
    first, last = stem_strips[0:1], stem_strips[5:6]
    near = lax.ppermute(jnp.where(even, last, first), both, STRIP_NEAR)
    far = lax.ppermute(jnp.where(even, first, last), both, STRIP_FAR)
    weights = (row(norm_scale), row(norm_shift), expand_weight, depth_weight, project_weight)
    middle, expanded = bottleneck_middle(
        *[pltpu.with_memory_space_constraint(a, pltpu.HBM) for a in (stem_strips, *weights)]
    )
    own_l, outer_l, inner_l = bottleneck_edge(stem_strips, near, far, expanded, middle, *weights)
    own_l, outer_l, inner_l, near, far = lax.optimization_barrier((own_l, outer_l, inner_l, near, far))
    outer_l = lax.ppermute(outer_l, "cols", Y_OUTER)
    inner_l = lax.ppermute(inner_l, "cols", Y_INNER)
    own_r, outer_r, inner_r = bottleneck_right(stem_strips, near, far, *weights)
    outer_l, inner_l, outer_r, inner_r = lax.optimization_barrier(
        (outer_l, inner_l, outer_r, inner_r)
    )
    outer_r = lax.ppermute(outer_r, "cols", Y_OUTER)
    inner_r = lax.ppermute(inner_r, "cols", Y_INNER)
    block_weights = (
        row(block_gain), block_inputs, block_output, block_bias,
        row(first_gain), first_up, first_down,
    )
    grid_weights = (
        row(grid_gain), grid_inputs, grid_output, grid_bias,
        row(second_gain), second_up, second_down,
    )
    left = block_section(0, own_l, outer_l, inner_l, block_weights)
    sent = block_section(1, own_r, outer_r, inner_r, block_weights, left)
    arrived = lax.all_to_all(sent, "rows", 0, 0, axis_index_groups=CORE_ROWS, tiled=True)
    back = grid_section(arrived, grid_weights)
    landed = lax.all_to_all(back, both, 0, 0, axis_index_groups=CORE_ALL, tiled=True)
    landed = landed.reshape(8, 2, 3, 4, 16, 256).transpose(1, 2, 0, 3, 4, 5)
    return landed.reshape(48, 64, 256)


def solution(mesh):
    return jax.shard_map(
        body,
        mesh=mesh,
        in_specs=(P(("rows", "cols"), None, None),) + (P(),) * 19,
        out_specs=P("rows", "cols", None),
        check_vma=False,
    )
```

```python
import functools

import jax
import jax.numpy as jnp
from jax import lax
from jax.experimental import pallas as pl
from jax.experimental.pallas import tpu as pltpu
from jax.sharding import PartitionSpec as P

EPSILON = 1e-05
LOG2E = 1.4426950408889634
GELU_A = 0.7978845608028654
GELU_B = GELU_A * 0.044715
F32 = jnp.float32
BF16 = jnp.bfloat16

CORE_ROWS = [[core + 2 * i for i in range(8)] for core in range(2)]
CORE_ALL = [[(core + 2 * i) * 8 + c for i in range(8) for c in range(8)] for core in range(2)]
Y_OUTER = [(c, c ^ 1) for c in range(8)]
Y_INNER = [(c, c // 4 * 4 + (0, 2, 1, 3)[c % 4]) for c in range(8)]
STRIP_NEAR = [(d, d ^ 1) for d in range(128)]
STRIP_FAR = [(d, ((d + 1) ^ 1) - 1 if 0 < d < 127 else 127 - d) for d in range(128)]


def twice_gelu(x):
    inner = x * (GELU_B * (x * x) + GELU_A)
    return x * (1.0 + jnp.tanh(inner))


def own_y():
    return lax.rem(lax.axis_index("cols"), 4)


PAD = 8
SPAN = 272
FIRST = (0, 240)


def twice_gelu_short(x):
    x = x.astype(BF16)
    inner = x * (BF16(GELU_B) * (x * x) + BF16(GELU_A))
    return x * (BF16(1.0) + jnp.tanh(inner))


def clear_edges(e_ref):
    edge = jnp.zeros((PAD, 128), F32)

    def clear(index, carry):
        for lb in range(8):
            e_ref[index, lb, 0:PAD, :] = edge
            e_ref[index, lb, SPAN + PAD : SPAN + 2 * PAD, :] = edge
        return carry

    lax.fori_loop(0, e_ref.shape[0], clear, 0)


def expand_row(values, scale, shift, we_ref, e_ref, row, factor):
    normed = (values.astype(F32) * scale + shift).astype(BF16)
    for nb in range(4):
        flat = jnp.dot(normed, we_ref[:, nb * 256 : (nb + 1) * 256], preferred_element_type=F32)
        wide = twice_gelu_short(flat).astype(F32)
        if factor is not None:
            wide = wide * factor
        for part in range(2):
            e_ref[row, nb * 2 + part, PAD : SPAN + PAD, :] = wide[:, part * 128 : (part + 1) * 128]


def depth_row(half, sources, values, taps, wp_ref, out_ref, at_row):
    base = 256 * half - FIRST[half] + PAD
    total = jnp.zeros((256, 256), F32)
    for pair in range(4):
        parts = []
        for lb in (2 * pair, 2 * pair + 1):
            acc = None
            for tap in range(9):
                e_ref, at = sources[tap // 3]
                term = (
                    e_ref[at, lb, pl.ds(base - 1 + tap % 3, 256), :]
                    * taps[tap : tap + 1, lb * 128 : (lb + 1) * 128]
                )
                acc = term if acc is None else acc + term
            parts.append(twice_gelu_short(acc))
        wide = jnp.concatenate(parts, axis=1)
        total = total + jnp.dot(
            wide, wp_ref[pair * 256 : (pair + 1) * 256, :], preferred_element_type=F32
        )
    result = (values.astype(F32) + 0.5 * total).astype(BF16)
    for jj in range(4):
        for tp in range(4):
            at = jj * 64 + tp * 16
            out_ref[at_row * 4 + tp, jj] = result[at : at + 16]


def middle_kernel(
    x_hbm, scale_hbm, shift_hbm, we_hbm, dw_hbm, wp_hbm, mid_ref, e_ref,
    x_ref, scale_ref, shift_ref, we_ref, dw_ref, wp_ref, sem,
):
    pairs = [(scale_hbm, scale_ref), (shift_hbm, shift_ref), (we_hbm, we_ref)]
    pairs += [(x_hbm.at[r, pl.ds(0, SPAN)], x_ref.at[r]) for r in range(6)]
    pairs += [(dw_hbm, dw_ref), (wp_hbm, wp_ref)]
    copies = [pltpu.make_async_copy(a, b, sem.at[n]) for n, (a, b) in enumerate(pairs)]
    for copy in copies:
        copy.start()
    clear_edges(e_ref)
    for copy in copies[:3]:
        copy.wait()
    scale, shift = scale_ref[...], shift_ref[...]
    for row in range(6):
        copies[3 + row].wait()
        expand_row(x_ref[row], scale, shift, we_ref, e_ref, row, None)
    for copy in copies[9:]:
        copy.wait()
    taps = dw_ref[...] * 0.5

    def depth(step, carry):
        for row in (2 * step + 1, 2 * step + 2):
            sources = [(e_ref, row - 1), (e_ref, row), (e_ref, row + 1)]
            depth_row(0, sources, x_ref[row, 0:256], taps, wp_ref, mid_ref, row - 1)
        return carry

    lax.fori_loop(0, 2, depth, 0)


def pick_pieces(own_ref, outer_ref, inner_ref):
    v = own_y()

    def pick(m, up):
        wide = jnp.where(up, v + 1, 4 - v)
        first = jnp.where(up, 2 * v, 0)
        row = jnp.minimum(first + m // wide, 5)
        tp = jnp.clip(jnp.where(up, 3 - v, 0) + lax.rem(m, wide), 0, 3)
        return own_ref[row * 4 + tp]

    def pick_outer(m, carry):
        outer_ref[m] = pick(m, lax.rem(v, 2) == 0)
        return carry

    def pick_inner(m, carry):
        inner_ref[m] = pick(m, v < 2)
        return carry

    lax.fori_loop(0, 6, pick_outer, 0)
    lax.fori_loop(0, 8, pick_inner, 0)


def expand_halo(half, near_ref, far_ref, scale, shift, we_ref, e_ref, rows):
    device = lax.axis_index("rows") * 8 + lax.axis_index("cols")
    even = lax.rem(device, 2) == 0
    cols = slice(FIRST[half], FIRST[half] + SPAN)
    above, below = rows
    row = jnp.where(even, below, above)
    expand_row(near_ref[0, cols], scale, shift, we_ref, e_ref, row, None)
    inside = jnp.logical_and(device > 0, device < 127).astype(F32)
    row = jnp.where(even, above, below)
    expand_row(far_ref[0, cols], scale, shift, we_ref, e_ref, row, inside)


def edge_kernel(
    x_ref, near_ref, far_ref, e_ref, mid_ref, scale_ref, shift_ref, we_ref, dw_ref, wp_ref,
    own_ref, outer_ref, inner_ref, halo_ref,
):
    clear_edges(halo_ref)
    expand_halo(0, near_ref, far_ref, scale_ref[...], shift_ref[...], we_ref, halo_ref, (0, 1))
    taps = dw_ref[...] * 0.5
    sources = [(halo_ref, 0), (e_ref, 0), (e_ref, 1)]
    depth_row(0, sources, x_ref[0, 0:256], taps, wp_ref, own_ref, 0)
    sources = [(e_ref, 4), (e_ref, 5), (halo_ref, 1)]
    depth_row(0, sources, x_ref[5, 0:256], taps, wp_ref, own_ref, 5)

    def keep(m, carry):
        own_ref[4 + m] = mid_ref[m]
        return carry

    lax.fori_loop(0, 16, keep, 0)
    pick_pieces(own_ref, outer_ref, inner_ref)


def right_kernel(
    x_ref, near_ref, far_ref, scale_ref, shift_ref, we_ref, dw_ref, wp_ref,
    own_ref, outer_ref, inner_ref, e_ref,
):
    clear_edges(e_ref)
    scale, shift = scale_ref[...], shift_ref[...]
    expand_halo(1, near_ref, far_ref, scale, shift, we_ref, e_ref, (0, 7))
    cols = slice(FIRST[1], FIRST[1] + SPAN)

    def expand(step, carry):
        for row in (3 * step, 3 * step + 1, 3 * step + 2):
            expand_row(x_ref[row, cols], scale, shift, we_ref, e_ref, row + 1, None)
        return carry

    lax.fori_loop(0, 2, expand, 0)
    taps = dw_ref[...] * 0.5

    def depth(step, carry):
        for row in (2 * step, 2 * step + 1):
            sources = [(e_ref, row), (e_ref, row + 1), (e_ref, row + 2)]
            depth_row(1, sources, x_ref[row, 256:512], taps, wp_ref, own_ref, row)
        return carry

    lax.fori_loop(0, 3, depth, 0)
    pick_pieces(own_ref, outer_ref, inner_ref)


def vmem(limit):
    return pltpu.CompilerParams(vmem_limit_bytes=limit * 1024 * 1024)


def pieces(count):
    return jax.ShapeDtypeStruct((count, 4, 16, 256), BF16)


def bottleneck_middle(strips, scale, shift, we, dw, wp):
    return pl.pallas_call(
        middle_kernel,
        out_shape=[pieces(16), jax.ShapeDtypeStruct((6, 8, SPAN + 2 * PAD, 128), F32)],
        in_specs=[pl.BlockSpec(memory_space=pltpu.HBM)] * 6,
        scratch_shapes=[
            pltpu.VMEM((6, SPAN, 256), BF16),
            pltpu.VMEM((1, 256), F32),
            pltpu.VMEM((1, 256), F32),
            pltpu.VMEM((256, 1024), BF16),
            pltpu.VMEM((9, 1024), F32),
            pltpu.VMEM((1024, 256), BF16),
            pltpu.SemaphoreType.DMA((11,)),
        ],
        compiler_params=vmem(24),
        name="bottleneck_middle",
    )(strips, scale, shift, we, dw, wp)


def bottleneck_edge(strips, near, far, expanded, middle, scale, shift, we, dw, wp):
    return pl.pallas_call(
        edge_kernel,
        out_shape=[pieces(24), pieces(6), pieces(8)],
        scratch_shapes=[pltpu.VMEM((2, 8, SPAN + 2 * PAD, 128), F32)],
        compiler_params=vmem(24),
        name="bottleneck_edge",
    )(strips, near, far, expanded, middle, scale, shift, we, dw, wp)


def bottleneck_right(strips, near, far, scale, shift, we, dw, wp):
    return pl.pallas_call(
        right_kernel,
        out_shape=[pieces(24), pieces(6), pieces(8)],
        scratch_shapes=[pltpu.VMEM((8, 8, SPAN + 2 * PAD, 128), F32)],
        compiler_params=vmem(24),
        name="bottleneck_right",
    )(strips, near, far, scale, shift, we, dw, wp)


def normed_of(x, gain):
    ones = jnp.full((256, 256), 1.0 / 256.0, BF16)
    center = x - jnp.dot(x.astype(BF16), ones, preferred_element_type=F32)
    squares = (center * center).astype(BF16)
    spread = jnp.dot(squares, ones, preferred_element_type=F32)
    return (center * lax.rsqrt(spread + EPSILON) * gain).astype(BF16)


def head_masks(dtype):
    lane = lax.broadcasted_iota(jnp.int32, (1, 128), 1)
    return [(lane // 32 == h).astype(F32).astype(dtype) for h in range(4)]


def attend_and_mix(x, w):
    tokens = x.shape[0]
    masks = head_masks(BF16)
    key_head = lax.broadcasted_iota(jnp.int32, (256, 128), 0) // 64
    lane_head = lax.broadcasted_iota(jnp.int32, (256, 128), 1) // 32
    head_ones = (key_head == lane_head).astype(F32).astype(BF16)
    score_lane = lax.broadcasted_iota(jnp.int32, (64, 256), 1)
    bias = [
        jnp.concatenate([w["bias"][4 * g + h] for h in range(4)], axis=1) * LOG2E
        for g in range(2)
    ]
    normed = normed_of(x, w["gain_a"][...])
    q, k, v = [
        jnp.dot(normed, w["inputs"][:, c * 256 : (c + 1) * 256], preferred_element_type=F32).astype(
            BF16
        )
        for c in range(3)
    ]
    rows = []
    for win in range(tokens // 64):
        at = slice(win * 64, (win + 1) * 64)
        groups = []
        for g in range(2):
            lanes = slice(g * 128, (g + 1) * 128)
            qg, kg, vg = q[at, lanes], k[at, lanes], v[at, lanes]
            keys = jnp.concatenate([kg * masks[h] for h in range(4)], axis=0)
            values = jnp.concatenate([vg * masks[h] for h in range(4)], axis=0)
            values = jnp.concatenate([values, head_ones], axis=1)
            scores = lax.dot_general(
                qg, keys, (((1,), (1,)), ((), ())), preferred_element_type=F32
            )
            scores = scores * (LOG2E * 32**-0.5) + bias[g]
            top = None
            for h in range(4):
                peak = jnp.max(scores[:, h * 64 : (h + 1) * 64], axis=1, keepdims=True)
                top = (
                    jnp.broadcast_to(peak, (64, 256))
                    if top is None
                    else jnp.where(score_lane >= h * 64, peak, top)
                )
            weights = jnp.exp2(scores - top).astype(BF16)
            mixed = jnp.dot(weights, values, preferred_element_type=F32)
            groups.append((mixed[:, :128] * (1.0 / mixed[:, 128:])).astype(BF16))
        rows.append(jnp.concatenate(groups, axis=1))
    combined = jnp.concatenate(rows, axis=0)
    x = x + jnp.dot(combined, w["output"][...], preferred_element_type=F32)
    x = x.astype(BF16).astype(F32)
    normed = normed_of(x, w["gain_m"][...])
    total = jnp.zeros((tokens, 256), F32)
    for c in range(4):
        cols = slice(c * 256, (c + 1) * 256)
        hidden = jnp.dot(normed, w["up"][:, cols], preferred_element_type=F32)
        hidden = twice_gelu_short(hidden)
        total = total + jnp.dot(hidden, w["down"][cols, :], preferred_element_type=F32)
    return x + 0.5 * total


NAMES = ("gain_a", "inputs", "output", "bias", "gain_m", "up", "down")


def block_places():
    y = own_y()
    places = []
    for k in range(3):
        n = 3 * y + k
        p = n // 4
        tp = lax.rem(n, 4)
        for s in range(8):
            row = 8 * p + s
            owner = row // 6
            local = row - 6 * owner
            v = jnp.maximum(y - 1, 0)
            m_up = (local - 2 * v) * (v + 1) + tp - (3 - v)
            v = jnp.minimum(y + 1, 3)
            m = jnp.where(owner < y, m_up, local * (4 - v) + tp)
            outer = owner // 2 == y // 2
            places.append((owner, local * 4 + tp, outer, jnp.clip(m, 0, 5), jnp.clip(m, 0, 7)))
    return y, places


def block_kernel(half, own_ref, outer_ref, inner_ref, *refs):
    w = dict(zip(NAMES, refs))
    refs = refs[len(NAMES) :]
    if half == 1:
        done_ref, out_ref = refs
        out_ref[:, :, 0:4] = done_ref[...]
    else:
        (out_ref,) = refs
    y, places = block_places()
    units = []
    for owner, at, outer, m_outer, m_inner in places:
        mine = own_ref[at].astype(F32)
        one = outer_ref[m_outer].astype(F32)
        two = inner_ref[m_inner].astype(F32)
        units.append(jnp.where(owner == y, mine, jnp.where(outer, one, two)))
    windows = [(k, jj, t) for k in range(3) for jj in range(4) for t in range(2)]
    x = jnp.concatenate(
        [units[k * 8 + s][jj, t * 8 : (t + 1) * 8, :] for k, jj, t in windows for s in range(8)],
        axis=0,
    )
    out = attend_and_mix(x, w)
    for k in range(3):
        for jj in range(4):
            first = (k * 4 + jj) * 128
            for s in range(8):
                both = [out[first + t * 64 + s * 8 :][:8] for t in range(2)]
                out_ref[s, k, jj + 4 * half] = jnp.concatenate(both, axis=0).astype(BF16)


def grid_kernel(x_ref, *refs):
    w = dict(zip(NAMES, refs))
    out_ref, flat_ref = refs[len(NAMES) :]

    def slot(k, carry):
        for i in range(8):
            values = x_ref[i, k].astype(F32).reshape(128, 256)
            for half in range(2):
                flat_ref[half, i * 128 : (i + 1) * 128, :] = values[
                    :, half * 128 : (half + 1) * 128
                ]
        windows = []
        for b in range(16):
            at = pl.ds(b, 64, stride=16)
            windows.append(
                jnp.concatenate([flat_ref[half, at, :] for half in range(2)], axis=1)
            )
        out = attend_and_mix(jnp.concatenate(windows, axis=0), w)
        for b in range(16):
            at = pl.ds(b, 64, stride=16)
            for half in range(2):
                flat_ref[half, at, :] = out[
                    b * 64 : (b + 1) * 64, half * 128 : (half + 1) * 128
                ]
        for i in range(8):
            values = jnp.concatenate(
                [flat_ref[half, i * 128 : (i + 1) * 128, :] for half in range(2)], axis=1
            )
            out_ref[pl.ds(i * 8, 8), k] = values.astype(BF16).reshape(8, 16, 256)
        return carry

    lax.fori_loop(0, 3, slot, 0)


def block_section(half, own, outer, inner, weights, *done):
    return pl.pallas_call(
        functools.partial(block_kernel, half),
        out_shape=jax.ShapeDtypeStruct((8, 3, 4 if half == 0 else 8, 16, 256), BF16),
        compiler_params=vmem(24),
        name="block_section",
    )(own, outer, inner, *weights, *done)


def grid_section(x, weights):
    return pl.pallas_call(
        grid_kernel,
        out_shape=jax.ShapeDtypeStruct((64, 3, 16, 256), BF16),
        scratch_shapes=[pltpu.VMEM((2, 1024, 128), F32)],
        compiler_params=vmem(24),
        name="grid_section",
    )(x, *weights)


def body(
    stem_strips, norm_scale, norm_shift, expand_weight, depth_weight, project_weight,
    block_gain, block_inputs, block_output, block_bias, first_gain, first_up, first_down,
    grid_gain, grid_inputs, grid_output, grid_bias, second_gain, second_up, second_down,
):
    row = lambda a: a.reshape(1, -1)
    both = ("rows", "cols")
    even = lax.rem(lax.axis_index("cols"), 2) == 0
    first, last = stem_strips[0:1], stem_strips[5:6]
    near = lax.ppermute(jnp.where(even, last, first), both, STRIP_NEAR)
    far = lax.ppermute(jnp.where(even, first, last), both, STRIP_FAR)
    weights = (row(norm_scale), row(norm_shift), expand_weight, depth_weight, project_weight)
    middle, expanded = bottleneck_middle(
        *[pltpu.with_memory_space_constraint(a, pltpu.HBM) for a in (stem_strips, *weights)]
    )
    own_l, outer_l, inner_l = bottleneck_edge(stem_strips, near, far, expanded, middle, *weights)
    own_l, outer_l, inner_l, near, far = lax.optimization_barrier((own_l, outer_l, inner_l, near, far))
    outer_l = lax.ppermute(outer_l, "cols", Y_OUTER)
    inner_l = lax.ppermute(inner_l, "cols", Y_INNER)
    own_r, outer_r, inner_r = bottleneck_right(stem_strips, near, far, *weights)
    outer_l, inner_l, outer_r, inner_r = lax.optimization_barrier(
        (outer_l, inner_l, outer_r, inner_r)
    )
    outer_r = lax.ppermute(outer_r, "cols", Y_OUTER)
    inner_r = lax.ppermute(inner_r, "cols", Y_INNER)
    block_weights = (
        row(block_gain), block_inputs, block_output, block_bias,
        row(first_gain), first_up, first_down,
    )
    grid_weights = (
        row(grid_gain), grid_inputs, grid_output, grid_bias,
        row(second_gain), second_up, second_down,
    )
    left = block_section(0, own_l, outer_l, inner_l, block_weights)
    sent = block_section(1, own_r, outer_r, inner_r, block_weights, left)
    arrived = lax.all_to_all(sent, "rows", 0, 0, axis_index_groups=CORE_ROWS, tiled=True)
    back = grid_section(arrived, grid_weights)
    landed = lax.all_to_all(back, both, 0, 0, axis_index_groups=CORE_ALL, tiled=True)
    landed = landed.reshape(8, 2, 3, 4, 16, 256).transpose(1, 2, 0, 3, 4, 5)
    return landed.reshape(48, 64, 256)


def solution(mesh):
    return jax.shard_map(
        body,
        mesh=mesh,
        in_specs=(P(("rows", "cols"), None, None),) + (P(),) * 19,
        out_specs=P("rows", "cols", None),
        check_vma=False,
    )
```
